128 devices in a mesh: dp: 8 (over z, core), expert: 16 (over y, x).
Axes of the slice: x: 4, y: 4, z: 4, core: 2. Of those that a mesh axis runs over, the one named last changes fastest.
Arguments:
- queries: bfloat16 [2048, 64, 576], P('dp', 'expert'), may hold values from -6 to 6
- cached_latent_rows: bfloat16 [2048, 8, 576], P('dp'), may hold values from -6 to 6
- lengths: int32 [2048], P('dp'), may hold values from 1 to 8, 8192 in all
- value_up_weight: bfloat16 [64, 512, 128], P('expert'), may hold values from -0.25 to 0.25
- out_proj: bfloat16 [8192, 3584], P('expert', 'dp'), may hold values from -0.0625 to 0.0625
- residual_in: bfloat16 [2048, 3584], P(('dp', 'expert')), may hold values from -6 to 6
- norm_gain: float32 [3584], replicated, may hold values from 0.25 to 1.75
- routes: int32 [2048, 8], P(('dp', 'expert')), may hold values from 0 to 127, all different within a row; in each aligned block of 16 rows (0 to 15, 16 to 31, ...) at most 2 rows name the same one
- route_scores: float32 [2048, 8], P(('dp', 'expert')), may hold values from 0.05 to 1
- w_gate_up: bfloat16 [128, 3584, 2048], P(('dp', 'expert')), may hold values from -0.09375 to 0.09375
- w_down: bfloat16 [128, 1024, 3584], P(('dp', 'expert')), may hold values from -0.1875 to 0.1875
Outputs:
- layer_out: bfloat16 [2048, 3584], P(('dp', 'expert'))
The draws below stay inside these ranges and needn't reach their ends.
Inputs may be any that keep to these rules, and one draw needn't show every extreme that they name: `routes`: the 8 experts of a request differ; among the 16 requests of one device (aligned blocks of rows) no expert is named more than 2 times, a bound that some block reaches.
All inputs are finite; a program needn't handle non-finite values. No bound on the sum of `lengths` on one device may be relied on, other than what follows from the above.
Results may differ from the reference program's by a relative error of at most 0.022.
Values may be sent and summed in bfloat16 or wider, within the bound.
No kernel may reach another device: no remote copies, remote signals or barrier semaphores. Data moves between devices by JAX's collectives and lax.ppermute only.
A program may use at most 128 MiB of HBM per device.

```python
import math
import jax
import jax.numpy as jnp
import numpy as np
from jax import lax

D = 3584
FF = 1024
HEAD_COUNT = 64
LATENT_WIDTH = 512
ROTARY_WIDTH = 64
VALUE_HEAD_WIDTH = 128
TOP = 8
REQ_DEV = 16
CACHE_LENGTH = 8
EXPERTS = 128
CAP = 2
REQUEST_TOTAL = 2048


def block_levels(stream_key, shape, shards, low, largest):
    factor_of, own = 1.0, jax.random.fold_in(stream_key, 6)
    for dim, shards_of in shards:
        draws = jnp.exp(jax.random.uniform(jax.random.fold_in(own, dim), (shards_of,), jnp.float32, low / len(shards), largest / len(shards)))
        factor_of = factor_of * jnp.repeat(draws, shape[dim] // shards_of).reshape([-1 if axis == dim else 1 for axis in range(len(shape))])
    return factor_of


def profile(amount, total, bound, slope):
    weights = [(1 << 20) // math.isqrt(grade ** slope) + 1 for grade in range(2, amount + 1)]
    spare, given = total - bound - (amount - 1), [1] * (amount - 1)
    while spare > 0:
        free = [i for i in range(amount - 1) if given[i] < bound]
        mass, budget = sum([weights[i] for i in free]), spare
        for i in free:
            more = min(bound - given[i], max(1, budget * weights[i] // mass), spare)
            given[i] = given[i] + more
            spare = spare - more
    return np.array([bound] + given)


def uneven(own_key, count, total, most, lean):
    if count == 2:
        one = jax.random.randint(own_key, (), max(1, total - most), min(most, total - 1) + 1)
        return jnp.stack([one, total - one])
    sizes = jnp.asarray(profile(count, total, most, lean), jnp.int32)
    pairs = (count - 1) // 2
    source_of, sink = sizes[1:1 + 2 * pairs:2], sizes[2:2 + 2 * pairs:2]
    margin = jnp.minimum(source_of - 1, most - sink)
    passed = jax.random.randint(jax.random.fold_in(own_key, 1), (pairs,), 0, 1 << 20) % (margin + 1)
    sizes = sizes.at[1:1 + 2 * pairs:2].set(source_of - passed).at[2:2 + 2 * pairs:2].set(sink + passed)
    return sizes[jax.random.permutation(jax.random.fold_in(own_key, 2), count)]


def routed_block(rng, own, number, rows, number_of, top, reach, skew):
    ranking = jax.random.permutation(rng, number_of)
    heavy_load, ordinary = portions_of(number_of, rows * top, reach, skew, True), portions_of(number_of, rows * top, reach, skew, False)
    places = jnp.arange(number_of)

    def named(sizes, offset_by):
        used = int((sizes > 0).sum())
        fixed = max(1, used // 4)
        passed = fixed + (places - fixed + offset_by * (used - fixed)) % max(1, number_of - fixed)
        return jnp.zeros((number_of,), jnp.int32).at[ranking[jnp.where(places < fixed, places, passed)]].set(jnp.asarray(sizes, jnp.int32))

    sizes = jnp.where(number % 4 == 0, named(heavy_load, number // 4), named(ordinary, number - number // 4 - 1))
    mixed = jax.random.permutation(jax.random.fold_in(own, 3), number_of)
    source_of, taker = mixed[0:number_of // 2 * 2:2], mixed[1:number_of // 2 * 2:2]
    slack = jnp.minimum(sizes[source_of] - 1, reach - sizes[taker]) // 2
    slack = jnp.where((source_of == ranking[0]) | (taker == ranking[0]) | (sizes[taker] == 0), 0, jnp.maximum(slack, 0))
    passed = jax.random.randint(jax.random.fold_in(own, 4), (number_of // 2,), 0, 1 << 20) % (slack + 1)
    sizes = sizes.at[source_of].add(-passed).at[taker].add(passed)
    labels = jnp.searchsorted(jnp.cumsum(sizes), jnp.arange(rows * top), side="right").astype(jnp.int32)
    grid = labels.reshape(top, rows).T
    grid = grid[jax.random.permutation(jax.random.fold_in(own, 1), rows)]
    offset_by = jax.random.randint(jax.random.fold_in(own, 2), (rows, 1), 0, top)
    return jnp.take_along_axis(grid, (jnp.arange(top)[None, :] + offset_by) % top, axis=1)


def portions_of(number_of, total, bound, slope, full):
    loads = [(1 << 20) // math.isqrt(grade ** slope) + 1 for grade in range(1, number_of + 1)]
    largest = bound if full else min(bound, max(-(-total // number_of), total * loads[0] // sum(loads)))
    least = 1 if total - largest >= number_of - 1 else 0
    holding, surplus = [largest] + [least] * (number_of - 1), total - largest - least * (number_of - 1)
    while surplus > 0:
        candidates = [i for i in range(1, number_of) if holding[i] < largest] or [i for i in range(1, number_of) if holding[i] < bound]
        mass, left = sum([loads[i] for i in candidates]), surplus
        for i in candidates:
            extra = min(bound - holding[i], max(1, left * loads[i] // mass), surplus)
            holding[i] = holding[i] + extra
            surplus = surplus - extra
    return np.array(holding)


def scatter_about(stream_key, shape, deviation, limit, pieces=(), kind=jnp.bfloat16):
    values = deviation * jax.random.normal(stream_key, shape, jnp.float32)
    if pieces:
        values = values * block_levels(stream_key, shape, pieces, -0.22, 0.18)
    return jnp.clip(values, -limit, limit).astype(kind)


def setup_inputs(seed: int = 0) -> dict:
    splits = jax.random.split(jax.random.key(seed), 12)
    queries = scatter_about(splits[0], (REQUEST_TOTAL, HEAD_COUNT, LATENT_WIDTH + ROTARY_WIDTH), 1.0, 6.0, ((0, 8), (1, 16)))
    cached_latent_rows = scatter_about(splits[1], (REQUEST_TOTAL, CACHE_LENGTH, LATENT_WIDTH + ROTARY_WIDTH), 1.0, 6.0, ((0, 8),))
    lengths = uneven(splits[2], REQUEST_TOTAL, REQUEST_TOTAL * CACHE_LENGTH // 2, CACHE_LENGTH, 2).astype(jnp.int32)
    value_up_weight = scatter_about(splits[3], (HEAD_COUNT, LATENT_WIDTH, VALUE_HEAD_WIDTH), LATENT_WIDTH ** -0.5, 0.25, ((0, 16),))
    out_proj = scatter_about(splits[4], (HEAD_COUNT * VALUE_HEAD_WIDTH, D), (HEAD_COUNT * VALUE_HEAD_WIDTH) ** -0.5, 0.0625, ((0, 16), (1, 8)))
    residual_in = scatter_about(splits[5], (REQUEST_TOTAL, D), 1.0, 6.0, ((0, 128),))
    norm_gain = jnp.clip(1.0 + 0.15 * jax.random.normal(splits[6], (D,), jnp.float32), 0.25, 1.75)
    routes_keys = jax.random.split(jax.random.fold_in(splits[7], 1), REQUEST_TOTAL // REQ_DEV)
    routes_turns = jax.random.permutation(jax.random.fold_in(splits[7], 3), REQUEST_TOTAL // REQ_DEV)
    routes = jax.vmap(lambda own, number: routed_block(jax.random.fold_in(splits[7], 2), own, number, REQ_DEV, EXPERTS, TOP, CAP, 2))(routes_keys, routes_turns).reshape((REQUEST_TOTAL, TOP))
    route_scores = jnp.clip(jnp.exp(math.log(1.0) - 2.9957323 * jax.random.uniform(splits[8], (REQUEST_TOTAL, TOP), jnp.float32) ** block_levels(splits[8], (REQUEST_TOTAL, TOP), ((0, 128),), -0.2, 0.2)), 0.05, 1.0)
    w_gate_up = scatter_about(splits[9], (EXPERTS, D, 2 * FF), D ** -0.5, 0.09375, ((0, 128),))
    w_down = scatter_about(splits[10], (EXPERTS, FF, D), FF ** -0.5, 0.1875, ((0, 128),))
    return {"queries": queries, "cached_latent_rows": cached_latent_rows, "lengths": lengths, "value_up_weight": value_up_weight, "out_proj": out_proj, "residual_in": residual_in, "norm_gain": norm_gain, "routes": routes, "route_scores": route_scores, "w_gate_up": w_gate_up, "w_down": w_down}


score_scale = 0.07216878364870323

def reference(queries, cached_latent_rows, lengths, value_up_weight, out_proj, residual_in, norm_gain, routes, route_scores, w_gate_up, w_down):
    query_f = queries.astype(jnp.float32)
    cache_float = cached_latent_rows.astype(jnp.float32)
    scores = jnp.einsum('thc,tsc->ths', query_f, cache_float) * score_scale
    position = jnp.arange(CACHE_LENGTH, dtype=jnp.int32)
    live = position[None, None, :] < lengths[:, None, None]
    scores = jnp.where(live, scores, jnp.float32(-1e+30))
    peak = lax.optimization_barrier(jnp.max(scores, axis=2, keepdims=True))
    expo = jnp.exp(scores - peak)
    attention_probabilities = (expo / lax.optimization_barrier(jnp.sum(expo, axis=2, keepdims=True))).astype(jnp.bfloat16)
    latent_output = jnp.einsum('ulj,ujv->ulv', attention_probabilities.astype(jnp.float32), cache_float[:, :, :LATENT_WIDTH]).astype(jnp.bfloat16)
    head_out = jnp.einsum('thc,hcv->thv', latent_output.astype(jnp.float32), value_up_weight.astype(jnp.float32)).astype(jnp.bfloat16)
    attention = jnp.dot(head_out.reshape(REQUEST_TOTAL, HEAD_COUNT * VALUE_HEAD_WIDTH), out_proj, preferred_element_type=jnp.float32).astype(jnp.bfloat16)
    hidden = (residual_in.astype(jnp.float32) + attention.astype(jnp.float32)).astype(jnp.bfloat16)
    hidden_f = hidden.astype(jnp.float32)
    inverse = lax.rsqrt(lax.optimization_barrier(jnp.mean(hidden_f * hidden_f, axis=1, keepdims=True)) + 1e-06)
    normed = (hidden_f * inverse * norm_gain[None, :]).astype(jnp.bfloat16)
    gates = 2.5 * route_scores / lax.optimization_barrier(jnp.sum(route_scores, axis=1, keepdims=True))

    def one_expert(total, index):
        weights = w_gate_up[index]
        both = jnp.dot(normed, weights, preferred_element_type=jnp.float32)
        act = (jax.nn.silu(both[:, :FF]) * both[:, FF:]).astype(jnp.bfloat16)
        result = jnp.dot(act, w_down[index], preferred_element_type=jnp.float32).astype(jnp.bfloat16)
        factor = lax.optimization_barrier(jnp.sum(jnp.where(routes == index, gates, jnp.float32(0.0)), axis=1))
        return (total + factor[:, None] * result.astype(jnp.float32), None)
    moe_sum, unused = lax.scan(one_expert, jnp.zeros((REQUEST_TOTAL, D), jnp.float32), jnp.arange(EXPERTS, dtype=jnp.int32))
    return (hidden_f + moe_sum).astype(jnp.bfloat16)
```

```python
import functools

import jax
import jax.numpy as jnp
from jax import lax
from jax.experimental import pallas as pl
from jax.experimental.pallas import tpu as pltpu
from jax.sharding import Mesh, PartitionSpec as P

D = 3584
FF = 1024
HEADS = 4
LATENT = 512
WIDTH = 576
VALUE = 128
SLOTS = 8
TOP = 8
EXPERTS = 128
ROWS = 16
REQUESTS = 256
QUARTER = D // 4
PIECES = EXPERTS * 8
COLUMNS = 448

score_scale = 0.07216878364870323

f32, bf16 = jnp.float32, jnp.bfloat16
VMEM_BYTES = 56 * 1024 * 1024


def iota(shape, dim):
    return lax.broadcasted_iota(jnp.int32, shape, dim)


def mm(a, b):
    return jnp.dot(a, b, preferred_element_type=f32)


def attention_kernel(q_ref, k_ref, len_ref, up_ref, out_ref, lat_ref):
    def score_step(i, sums):
        rows = pl.ds(i * 16, 16)
        q = [q_ref[h, rows, :].astype(f32) for h in range(HEADS)]
        k = [k_ref[s, rows, :].astype(f32) for s in range(SLOTS)]
        new = []
        for h in range(HEADS):
            for s in range(SLOTS):
                prod = q[h] * k[s]
                new.append(sums[h * SLOTS + s] + (prod[:8] + prod[8:]))
        return tuple(new)

    sums = lax.fori_loop(
        0, WIDTH // 16, score_step, tuple(jnp.zeros((8, 128), f32) for _ in range(HEADS * SLOTS))
    )
    live = iota((SLOTS, 128), 0) < len_ref[...]
    probs = []
    for h in range(HEADS):
        scores = jnp.concatenate(
            [jnp.sum(sums[h * SLOTS + s], axis=0, keepdims=True) for s in range(SLOTS)], axis=0
        )
        scores = jnp.where(live, scores * score_scale, -1e30)
        expo = jnp.exp(scores - jnp.max(scores, axis=0, keepdims=True))
        prob = (expo / jnp.sum(expo, axis=0, keepdims=True)).astype(bf16).astype(f32)
        probs.append([jnp.broadcast_to(prob[s : s + 1], (8, 128)) for s in range(SLOTS)])

    @pl.loop(0, LATENT // 16)
    def _(i):
        rows = pl.ds(i * 16, 16)
        k = [k_ref[s, rows, :].astype(f32) for s in range(SLOTS)]
        for h in range(HEADS):
            low = sum(probs[h][s] * k[s][:8] for s in range(SLOTS))
            high = sum(probs[h][s] * k[s][8:] for s in range(SLOTS))
            lat_ref[h, rows, :] = jnp.concatenate([low, high], axis=0).astype(bf16)

    for h in range(HEADS):
        out_ref[:, h * VALUE : (h + 1) * VALUE] = lax.dot_general(
            lat_ref[h], up_ref[h], (((0,), (0,)), ((), ())), preferred_element_type=f32
        ).astype(bf16)


def attention(q, k, lengths, up):
    return pl.pallas_call(
        attention_kernel,
        grid=(REQUESTS // 128,),
        in_specs=[
            pl.BlockSpec((HEADS, WIDTH, 128), lambda j: (0, 0, j)),
            pl.BlockSpec((SLOTS, WIDTH, 128), lambda j: (0, 0, j)),
            pl.BlockSpec((1, 128), lambda j: (0, j)),
            pl.BlockSpec((HEADS, LATENT, VALUE), lambda j: (0, 0, 0)),
        ],
        out_specs=pl.BlockSpec((128, HEADS * VALUE), lambda j: (j, 0)),
        out_shape=jax.ShapeDtypeStruct((REQUESTS, HEADS * VALUE), bf16),
        scratch_shapes=[pltpu.VMEM((HEADS, LATENT, 128), bf16)],
        compiler_params=pltpu.CompilerParams(vmem_limit_bytes=VMEM_BYTES),
        cost_estimate=pl.CostEstimate(flops=40_000_000, bytes_accessed=4_200_000, transcendentals=8192),
        name="attention",
    )(q, k, lengths, up)


def plan_kernel(routes_ref, routes_t_ref, score_ref, place_ref, weight_ref):
    routes_t = routes_t_ref[...]
    named_t = jnp.zeros((EXPERTS, ROWS), f32)
    for k in range(TOP):
        named_t += (iota((EXPERTS, ROWS), 0) == routes_t[k : k + 1, :]).astype(f32)
    before_t = (iota((ROWS, ROWS), 0) < iota((ROWS, ROWS), 1)).astype(bf16)
    rank_t = mm(named_t.astype(bf16), before_t)
    spread = (iota((ROWS, 4 * ROWS), 1) % ROWS == iota((ROWS, 4 * ROWS), 0)).astype(bf16)
    expand = (iota((PIECES, EXPERTS), 0) // 8 == iota((PIECES, EXPERTS), 1)).astype(bf16)
    both = []
    for slot in range(2):
        here = jnp.where(rank_t == slot, named_t, 0.0).astype(bf16)
        both.append(mm(expand, mm(here, spread).astype(bf16)))
    n = iota((PIECES, 4 * ROWS), 0)
    place = jnp.where(n % 2 == 0, both[0], both[1])
    place_ref[...] = jnp.where(n % 8 // 2 == iota((PIECES, 4 * ROWS), 1) // ROWS, place, 0.0).astype(bf16)

    routes, scores = routes_ref[...], score_ref[...]
    gates = 2.5 * scores / jnp.sum(scores, axis=1, keepdims=True)
    named = jnp.zeros((ROWS, EXPERTS), f32)
    gate = jnp.zeros((ROWS, EXPERTS), f32)
    for k in range(TOP):
        hit = iota((ROWS, EXPERTS), 1) == routes[:, k : k + 1]
        named += hit.astype(f32)
        gate += jnp.where(hit, gates[:, k : k + 1], 0.0)
    before = (iota((ROWS, ROWS), 1) < iota((ROWS, ROWS), 0)).astype(bf16)
    rank = mm(before, named.astype(bf16))
    expand = (iota((EXPERTS, PIECES), 1) // 8 == iota((EXPERTS, PIECES), 0)).astype(bf16)
    n = iota((ROWS, PIECES), 1)
    high, low = [], []
    for slot in range(2):
        part = jnp.where(rank == slot, gate, 0.0)
        top = part.astype(bf16)
        high.append(mm(top, expand))
        low.append(mm((part - top.astype(f32)).astype(bf16), expand))
    for i, parts in enumerate((high, low)):
        row = jnp.where(n % 2 == 0, parts[0], parts[1])
        for quarter in range(4):
            weight_ref[pl.ds((i * 4 + quarter) * ROWS, ROWS), :] = jnp.where(
                n % 8 // 2 == quarter, row, 0.0
            ).astype(bf16)


def plan(routes, scores):
    return pl.pallas_call(
        plan_kernel,
        out_shape=(
            jax.ShapeDtypeStruct((PIECES, 4 * ROWS), bf16),
            jax.ShapeDtypeStruct((8 * ROWS, PIECES), bf16),
        ),
        compiler_params=pltpu.CompilerParams(vmem_limit_bytes=VMEM_BYTES),
        cost_estimate=pl.CostEstimate(flops=60_000_000, bytes_accessed=500_000, transcendentals=0),
        name="plan",
    )(routes, routes.T, scores)


def project_kernel(chip_ref, head_ref, *refs):
    blocks, out_ref, w_ref, sems = refs[:8], refs[8], refs[9], refs[10]
    z, core = chip_ref[0], chip_ref[1]

    def copy(i):
        chip = lax.rem(z + i // 2, 4)
        which = core if i % 2 == 0 else 1 - core
        start = pl.multiple_of((chip * 2 + which) * COLUMNS, 16)
        return pltpu.make_async_copy(blocks[i], w_ref.at[pl.ds(start, COLUMNS), :], sems.at[i])

    for i in range(8):
        copy(i).start()
    for step in range(4):
        copy(2 * step).wait()
        copy(2 * step + 1).wait()
        start = pl.multiple_of(lax.rem(z + step, 4) * QUARTER, 128)
        out_ref[:, pl.ds(start, QUARTER)] = lax.dot_general(
            head_ref[...],
            w_ref[pl.ds(start, QUARTER), :],
            (((1,), (1,)), ((), ())),
            preferred_element_type=f32,
        ).astype(bf16)


def project(chip, head_out, blocks):
    return pl.pallas_call(
        project_kernel,
        in_specs=[pl.BlockSpec(memory_space=pltpu.SMEM), pl.BlockSpec(memory_space=pltpu.VMEM)]
        + [pl.BlockSpec(memory_space=pl.ANY)] * 8,
        out_specs=pl.BlockSpec(memory_space=pltpu.VMEM),
        out_shape=jax.ShapeDtypeStruct((REQUESTS, D), bf16),
        scratch_shapes=[pltpu.VMEM((D, HEADS * VALUE), bf16), pltpu.SemaphoreType.DMA((8,))],
        compiler_params=pltpu.CompilerParams(vmem_limit_bytes=VMEM_BYTES),
        cost_estimate=pl.CostEstimate(flops=2 * REQUESTS * 512 * D, bytes_accessed=5_800_000, transcendentals=0),
        name="project",
    )(chip, head_out, *blocks)


def dispatch_kernel(parts_ref, res_ref, gain_ref, place_ref, hidden_ref, out_ref, norm_ref):
    total = parts_ref[0].astype(f32)
    for i in range(1, parts_ref.shape[0]):
        total += parts_ref[i].astype(f32)
    hidden = (res_ref[...].astype(f32) + total.astype(bf16).astype(f32)).astype(bf16)
    hidden_ref[...] = hidden
    hidden = hidden.astype(f32)
    inverse = lax.rsqrt(jnp.mean(hidden * hidden, axis=1, keepdims=True) + 1e-6)
    normed = (hidden * inverse * gain_ref[...]).astype(bf16)
    for quarter in range(4):
        norm_ref[pl.ds(quarter * ROWS, ROWS), :] = normed[:, quarter * QUARTER : (quarter + 1) * QUARTER]

    @pl.loop(0, 4)
    def _(i):
        rows = pl.ds(i * (PIECES // 4), PIECES // 4)
        out_ref[rows, :] = mm(place_ref[rows, :], norm_ref[...]).astype(bf16)


def dispatch(parts, residual, gain, place):
    return pl.pallas_call(
        dispatch_kernel,
        out_shape=(
            jax.ShapeDtypeStruct((ROWS, D), bf16),
            jax.ShapeDtypeStruct((PIECES, QUARTER), bf16),
        ),
        scratch_shapes=[pltpu.VMEM((4 * ROWS, QUARTER), bf16)],
        compiler_params=pltpu.CompilerParams(vmem_limit_bytes=VMEM_BYTES),
        cost_estimate=pl.CostEstimate(flops=120_000_000, bytes_accessed=4_000_000, transcendentals=16),
        name="dispatch",
    )(parts, residual, gain, place)


def expert_kernel(x_ref, wi_ref, wo_ref, out_ref, rows_ref, act_ref, back_ref, wi_buf, wo_buf, sems):
    half = FF // 4

    def copy_in(i):
        return pltpu.make_async_copy(
            wi_ref.at[:, pl.ds((i % 2) * FF + (i // 2) * half, half)], wi_buf.at[i], sems.at[i]
        )

    def copy_out(i):
        return pltpu.make_async_copy(
            wo_ref.at[:, pl.ds(i * QUARTER, QUARTER)], wo_buf.at[i], sems.at[8 + i]
        )

    for i in range(8):
        copy_in(i).start()
    for i in range(4):
        copy_out(i).start()

    def matches(to, frm):
        same_quarter = to // 64 == frm % 8 // 2
        return (same_quarter & (to % 64 // 2 == frm // 8) & (to % 2 == frm % 2)).astype(bf16)

    sort = matches(iota((256, 256), 0), iota((256, 256), 1))
    unsort = matches(iota((256, 256), 1), iota((256, 256), 0))
    for b in range(4):
        sorted_rows = mm(sort, x_ref[b * 256 : (b + 1) * 256, :]).astype(bf16)
        for quarter in range(4):
            rows_ref[b * 64 : (b + 1) * 64, quarter * QUARTER : (quarter + 1) * QUARTER] = sorted_rows[
                quarter * 64 : (quarter + 1) * 64
            ]

    for i in range(4):
        copy_in(2 * i).wait()
        copy_in(2 * i + 1).wait()
        gate = mm(rows_ref[...], wi_buf[2 * i])
        up = mm(rows_ref[...], wi_buf[2 * i + 1])
        act_ref[:, i * half : (i + 1) * half] = (jax.nn.silu(gate) * up).astype(bf16)

    for quarter in range(4):
        copy_out(quarter).wait()
        result = mm(act_ref[...], wo_buf[quarter]).astype(bf16)
        for b in range(4):
            back_ref[b, quarter * 64 : (quarter + 1) * 64, :] = result[b * 64 : (b + 1) * 64]
    for b in range(4):
        out_ref[b * 256 : (b + 1) * 256, :] = mm(unsort, back_ref[b]).astype(bf16)


def expert(pieces, w_in, w_out):
    rows = 2 * EXPERTS
    return pl.pallas_call(
        expert_kernel,
        in_specs=[
            pl.BlockSpec(memory_space=pltpu.VMEM),
            pl.BlockSpec(memory_space=pl.ANY),
            pl.BlockSpec(memory_space=pl.ANY),
        ],
        out_specs=pl.BlockSpec(memory_space=pltpu.VMEM),
        out_shape=jax.ShapeDtypeStruct((PIECES, QUARTER), bf16),
        scratch_shapes=[
            pltpu.VMEM((rows, D), bf16),
            pltpu.VMEM((rows, FF), bf16),
            pltpu.VMEM((4, 256, QUARTER), bf16),
            pltpu.VMEM((8, D, FF // 4), bf16),
            pltpu.VMEM((4, FF, QUARTER), bf16),
            pltpu.SemaphoreType.DMA((12,)),
        ],
        compiler_params=pltpu.CompilerParams(vmem_limit_bytes=VMEM_BYTES),
        cost_estimate=pl.CostEstimate(
            flops=2 * rows * 3 * D * FF, bytes_accessed=26_000_000, transcendentals=rows * FF
        ),
        name="expert",
    )(pieces, w_in, w_out)


def combine_kernel(back_ref, weight_ref, hidden_ref, out_ref):
    both = mm(weight_ref[...], back_ref[...])
    for quarter in range(4):
        columns = slice(quarter * QUARTER, (quarter + 1) * QUARTER)
        rows = slice(quarter * ROWS, (quarter + 1) * ROWS)
        low_rows = slice((4 + quarter) * ROWS, (5 + quarter) * ROWS)
        out_ref[:, columns] = (hidden_ref[:, columns].astype(f32) + (both[rows] + both[low_rows])).astype(bf16)


def combine(back, weight, hidden):
    return pl.pallas_call(
        combine_kernel,
        out_shape=jax.ShapeDtypeStruct((ROWS, D), bf16),
        compiler_params=pltpu.CompilerParams(vmem_limit_bytes=VMEM_BYTES),
        cost_estimate=pl.CostEstimate(flops=240_000_000, bytes_accessed=2_400_000, transcendentals=0),
        name="combine",
    )(back, weight, hidden)


def local(
    queries,
    cached_latent_rows,
    lengths,
    value_up_weight,
    out_proj,
    residual_in,
    norm_gain,
    routes,
    route_scores,
    w_gate_up,
    w_down,
):
    own = out_proj.T
    blocks = [own] + [
        lax.ppermute(own, "z", [(i, (i - step) % 4) for i in range(4)]) for step in (1, 2, 3)
    ]
    pairs = []
    for block in blocks:
        pairs += [block, lax.ppermute(block, "core", [(0, 1), (1, 0)])]
    chip = jnp.stack([lax.axis_index("z"), lax.axis_index("core")]).astype(jnp.int32)

    head_out = attention(
        queries.transpose(1, 2, 0),
        cached_latent_rows.transpose(1, 2, 0),
        lengths.reshape(1, REQUESTS),
        value_up_weight,
    )
    place, weight = plan(routes, route_scores)
    shares = project(chip, head_out, pairs)
    parts = lax.all_to_all(
        shares.reshape(16, ROWS, D), ("y", "x"), split_axis=0, concat_axis=0, tiled=True
    )
    hidden, outgoing = dispatch(parts, residual_in, norm_gain.reshape(1, D), place)
    everyone = ("z", "core", "y", "x")
    arrived = lax.all_to_all(
        outgoing.reshape(EXPERTS, 8, QUARTER), everyone, split_axis=0, concat_axis=0, tiled=True
    )
    produced = expert(arrived.reshape(PIECES, QUARTER), w_gate_up[0], w_down[0])
    returned = lax.all_to_all(
        produced.reshape(EXPERTS, 8, QUARTER), everyone, split_axis=0, concat_axis=0, tiled=True
    )
    return combine(returned.reshape(PIECES, QUARTER), weight, hidden)


def solution(mesh):
    fine = Mesh(mesh.devices.reshape(4, 2, 4, 4), ("z", "core", "y", "x"))
    dp, ex, both = ("z", "core"), ("y", "x"), ("z", "core", "y", "x")
    in_specs = (
        P(dp, ex, None),
        P(dp, None, None),
        P(dp),
        P(ex, None, None),
        P(ex, dp),
        P(both, None),
        P(),
        P(both, None),
        P(both, None),
        P(both, None, None),
        P(both, None, None),
    )
    return jax.shard_map(local, mesh=fine, in_specs=in_specs, out_specs=P(both, None), check_vma=False)
```

```python
import functools

import jax
import jax.numpy as jnp
from jax import lax
from jax.experimental import pallas as pl
from jax.experimental.pallas import tpu as pltpu
from jax.sharding import Mesh, PartitionSpec as P

D = 3584
FF = 1024
HEADS = 4
LATENT = 512
WIDTH = 576
VALUE = 128
SLOTS = 8
TOP = 8
EXPERTS = 128
ROWS = 16
REQUESTS = 256
QUARTER = D // 4
PIECES = EXPERTS * 8
COLUMNS = 448
STEPS, DEPTH = 7, D // 7

score_scale = 0.07216878364870323

f32, bf16 = jnp.float32, jnp.bfloat16
VMEM_BYTES = 16 * 1024 * 1024


def iota(shape, dim):
    return lax.broadcasted_iota(jnp.int32, shape, dim)


def mm(a, b):
    return jnp.dot(a, b, preferred_element_type=f32)


def attention_kernel(q_ref, k_ref, len_ref, up_ref, out_ref, lat_ref):
    def score_step(i, sums):
        rows = pl.ds(i * 16, 16)
        q = [q_ref[h, rows, :].astype(f32) for h in range(HEADS)]
        k = [k_ref[s, rows, :].astype(f32) for s in range(SLOTS)]
        new = []
        for h in range(HEADS):
            for s in range(SLOTS):
                prod = q[h] * k[s]
                new.append(sums[h * SLOTS + s] + (prod[:8] + prod[8:]))
        return tuple(new)

    sums = lax.fori_loop(
        0, WIDTH // 16, score_step, tuple(jnp.zeros((8, 128), f32) for _ in range(HEADS * SLOTS))
    )
    live = iota((SLOTS, 128), 0) < len_ref[...]
    probs = []
    for h in range(HEADS):
        scores = jnp.concatenate(
            [jnp.sum(sums[h * SLOTS + s], axis=0, keepdims=True) for s in range(SLOTS)], axis=0
        )
        scores = jnp.where(live, scores * score_scale, -1e30)
        expo = jnp.exp(scores - jnp.max(scores, axis=0, keepdims=True))
        prob = (expo / jnp.sum(expo, axis=0, keepdims=True)).astype(bf16).astype(f32)
        probs.append([jnp.broadcast_to(prob[s : s + 1], (8, 128)) for s in range(SLOTS)])

    @pl.loop(0, LATENT // 16)
    def _(i):
        rows = pl.ds(i * 16, 16)
        k = [k_ref[s, rows, :].astype(f32) for s in range(SLOTS)]
        for h in range(HEADS):
            low = sum(probs[h][s] * k[s][:8] for s in range(SLOTS))
            high = sum(probs[h][s] * k[s][8:] for s in range(SLOTS))
            lat_ref[h, rows, :] = jnp.concatenate([low, high], axis=0).astype(bf16)

    for h in range(HEADS):
        out_ref[:, h * VALUE : (h + 1) * VALUE] = lax.dot_general(
            lat_ref[h], up_ref[h], (((0,), (0,)), ((), ())), preferred_element_type=f32
        ).astype(bf16)


def attention(q, k, lengths, up):
    return pl.pallas_call(
        attention_kernel,
        grid=(REQUESTS // 128,),
        in_specs=[
            pl.BlockSpec((HEADS, WIDTH, 128), lambda j: (0, 0, j)),
            pl.BlockSpec((SLOTS, WIDTH, 128), lambda j: (0, 0, j)),
            pl.BlockSpec((1, 128), lambda j: (0, j)),
            pl.BlockSpec((HEADS, LATENT, VALUE), lambda j: (0, 0, 0)),
        ],
        out_specs=pl.BlockSpec((128, HEADS * VALUE), lambda j: (j, 0)),
        out_shape=jax.ShapeDtypeStruct((REQUESTS, HEADS * VALUE), bf16),
        scratch_shapes=[pltpu.VMEM((HEADS, LATENT, 128), bf16)],
        compiler_params=pltpu.CompilerParams(vmem_limit_bytes=VMEM_BYTES),
        cost_estimate=pl.CostEstimate(flops=9_000_000_000, bytes_accessed=4_200_000, transcendentals=8192),
        name="attention",
    )(q, k, lengths, up)


def plan_kernel(routes_ref, routes_t_ref, score_ref, place_ref, weight_ref):
    routes_t = routes_t_ref[...]
    named_t = jnp.zeros((EXPERTS, ROWS), f32)
    for k in range(TOP):
        named_t += (iota((EXPERTS, ROWS), 0) == routes_t[k : k + 1, :]).astype(f32)
    before_t = (iota((ROWS, ROWS), 0) < iota((ROWS, ROWS), 1)).astype(bf16)
    rank_t = mm(named_t.astype(bf16), before_t)
    spread = (iota((ROWS, 4 * ROWS), 1) % ROWS == iota((ROWS, 4 * ROWS), 0)).astype(bf16)
    expand = (iota((PIECES, EXPERTS), 0) // 8 == iota((PIECES, EXPERTS), 1)).astype(bf16)
    both = []
    for slot in range(2):
        here = jnp.where(rank_t == slot, named_t, 0.0).astype(bf16)
        both.append(mm(expand, mm(here, spread).astype(bf16)))
    n = iota((PIECES, 4 * ROWS), 0)
    place = jnp.where(n % 2 == 0, both[0], both[1])
    place_ref[...] = jnp.where(n % 8 // 2 == iota((PIECES, 4 * ROWS), 1) // ROWS, place, 0.0).astype(bf16)

    routes, scores = routes_ref[...], score_ref[...]
    gates = 2.5 * scores / jnp.sum(scores, axis=1, keepdims=True)
    named = jnp.zeros((ROWS, EXPERTS), f32)
    gate = jnp.zeros((ROWS, EXPERTS), f32)
    for k in range(TOP):
        hit = iota((ROWS, EXPERTS), 1) == routes[:, k : k + 1]
        named += hit.astype(f32)
        gate += jnp.where(hit, gates[:, k : k + 1], 0.0)
    before = (iota((ROWS, ROWS), 1) < iota((ROWS, ROWS), 0)).astype(bf16)
    rank = mm(before, named.astype(bf16))
    expand = (iota((EXPERTS, PIECES), 1) // 8 == iota((EXPERTS, PIECES), 0)).astype(bf16)
    n = iota((ROWS, PIECES), 1)
    high, low = [], []
    for slot in range(2):
        part = jnp.where(rank == slot, gate, 0.0)
        top = part.astype(bf16)
        high.append(mm(top, expand))
        low.append(mm((part - top.astype(f32)).astype(bf16), expand))
    for i, parts in enumerate((high, low)):
        row = jnp.where(n % 2 == 0, parts[0], parts[1])
        for quarter in range(4):
            weight_ref[pl.ds((i * 4 + quarter) * ROWS, ROWS), :] = jnp.where(
                n % 8 // 2 == quarter, row, 0.0
            ).astype(bf16)


def plan(routes, scores):
    return pl.pallas_call(
        plan_kernel,
        out_shape=(
            jax.ShapeDtypeStruct((PIECES, 4 * ROWS), bf16),
            jax.ShapeDtypeStruct((8 * ROWS, PIECES), bf16),
        ),
        compiler_params=pltpu.CompilerParams(vmem_limit_bytes=VMEM_BYTES),
        cost_estimate=pl.CostEstimate(flops=60_000_000, bytes_accessed=500_000, transcendentals=0),
        name="plan",
    )(routes, routes.T, scores)


def hold_kernel(next_ref, last_ref, after_ref, next_out, last_out):
    next_out[...] = next_ref[...]
    last_out[...] = last_ref[...]


def hold(next_block, last_block, after):
    block = jax.ShapeDtypeStruct((COLUMNS, HEADS * VALUE), bf16)
    whole = pl.BlockSpec((COLUMNS, HEADS * VALUE), lambda i: (0, 0))
    return pl.pallas_call(
        hold_kernel,
        grid=(1,),
        in_specs=[whole, whole, pl.BlockSpec((16, 128), lambda i: (0, 0))],
        out_specs=[whole, whole],
        out_shape=[block, block],
        compiler_params=pltpu.CompilerParams(vmem_limit_bytes=VMEM_BYTES),
        cost_estimate=pl.CostEstimate(flops=0, bytes_accessed=2_000_000, transcendentals=0),
        name="hold",
    )(next_block, last_block, after)


def project_kernel(first, chips, at_ref, head_ref, *refs):
    blocks, outs, (rows_ref, w_ref) = refs[: 2 * chips], refs[2 * chips : 2 * chips + 4], refs[2 * chips + 4 :]
    y, x, core = at_ref[1], at_ref[2], at_ref[3]
    for step in range(4):
        for other in range(4):
            if first == "x":
                start = other * 64 + lax.rem(x + step, 4) * ROWS
            else:
                start = lax.rem(y + step, 4) * 64 + other * ROWS
            rows_ref[pl.ds(step * 64 + other * ROWS, ROWS), :] = head_ref[
                pl.ds(pl.multiple_of(start, ROWS), ROWS), :
            ]
    for i in range(chips):
        own = pl.multiple_of(core * COLUMNS, 16)
        other = pl.multiple_of((1 - core) * COLUMNS, 16)
        w_ref[i, pl.ds(own, COLUMNS), :] = blocks[2 * i][...]
        w_ref[i, pl.ds(other, COLUMNS), :] = blocks[2 * i + 1][...]
        result = lax.dot_general(
            rows_ref[...], w_ref[i], (((1,), (1,)), ((), ())), preferred_element_type=f32
        ).astype(bf16)
        for step in range(4):
            outs[step][:, i * QUARTER : (i + 1) * QUARTER] = result[step * 64 : (step + 1) * 64]


def project(first, at, head_out, blocks):
    chips = len(blocks) // 2
    return pl.pallas_call(
        functools.partial(project_kernel, first, chips),
        in_specs=[pl.BlockSpec(memory_space=pltpu.SMEM)]
        + [pl.BlockSpec(memory_space=pltpu.VMEM)] * (1 + 2 * chips),
        out_shape=[jax.ShapeDtypeStruct((64, chips * QUARTER), bf16)] * 4,
        scratch_shapes=[
            pltpu.VMEM((REQUESTS, HEADS * VALUE), bf16),
            pltpu.VMEM((chips, QUARTER, HEADS * VALUE), bf16),
        ],
        compiler_params=pltpu.CompilerParams(vmem_limit_bytes=VMEM_BYTES),
        cost_estimate=pl.CostEstimate(
            flops=chips * REQUESTS * 512 * QUARTER * 2, bytes_accessed=chips * 1_500_000, transcendentals=0
        ),
        name="project_" + first,
    )(at, head_out, *blocks)


def reduce_kernel(second, place_ref, *refs):
    parts, outs = refs[:4], refs[4:]
    me = place_ref[1] if second == "y" else place_ref[2]
    for step in range(4):
        rows = pl.ds(pl.multiple_of(lax.rem(me + step, 4) * ROWS, ROWS), ROWS)
        total = parts[0][rows, :].astype(f32)
        for part in parts[1:]:
            total += part[rows, :].astype(f32)
        outs[step][...] = total.astype(bf16)


def reduce(second, place, parts):
    return pl.pallas_call(
        functools.partial(reduce_kernel, second),
        in_specs=[pl.BlockSpec(memory_space=pltpu.SMEM)] + [pl.BlockSpec(memory_space=pltpu.VMEM)] * 4,
        out_shape=[jax.ShapeDtypeStruct((ROWS, parts[0].shape[1]), bf16)] * 4,
        compiler_params=pltpu.CompilerParams(vmem_limit_bytes=VMEM_BYTES),
        cost_estimate=pl.CostEstimate(flops=500_000, bytes_accessed=1_200_000, transcendentals=0),
        name="reduce_" + second,
    )(place, *parts)


def total_kernel(*refs):
    total = refs[0][...].astype(f32)
    for part in refs[1:4]:
        total += part[...].astype(f32)
    refs[4][...] = total.astype(bf16)


def total(parts):
    return pl.pallas_call(
        total_kernel,
        out_shape=jax.ShapeDtypeStruct(parts[0].shape, bf16),
        compiler_params=pltpu.CompilerParams(vmem_limit_bytes=VMEM_BYTES),
        cost_estimate=pl.CostEstimate(flops=100_000, bytes_accessed=200_000, transcendentals=0),
        name="total",
    )(*parts)


def exchange(axis, parts):
    return [parts[0]] + [
        lax.ppermute(parts[step], axis, [(i, (i + step) % 4) for i in range(4)]) for step in (1, 2, 3)
    ]


def dispatch_kernel(at_ref, *refs):
    parts, (res_ref, gain_ref, place_ref, hidden_ref, out_ref, norm_ref, sum_ref) = refs[:5], refs[5:]
    z = at_ref[0]
    near = parts[0][...].astype(f32)
    for part in parts[1:4]:
        near += part[...].astype(f32)
    far = parts[4][...].astype(f32)
    for i, step in enumerate((0, 1, 3, 2)):
        start = pl.multiple_of(lax.rem(z + step, 4) * QUARTER, 128)
        sum_ref[:, pl.ds(start, QUARTER)] = near[:, i * QUARTER : (i + 1) * QUARTER] if i < 3 else far
    hidden = (res_ref[...].astype(f32) + sum_ref[...].astype(bf16).astype(f32)).astype(bf16)
    hidden_ref[...] = hidden
    hidden = hidden.astype(f32)
    inverse = lax.rsqrt(jnp.mean(hidden * hidden, axis=1, keepdims=True) + 1e-6)
    normed = (hidden * inverse * gain_ref[...]).astype(bf16)
    for quarter in range(4):
        norm_ref[pl.ds(quarter * ROWS, ROWS), :] = normed[:, quarter * QUARTER : (quarter + 1) * QUARTER]

    @pl.loop(0, 4)
    def _(i):
        rows = pl.ds(i * (PIECES // 4), PIECES // 4)
        out_ref[rows, :] = mm(place_ref[rows, :], norm_ref[...]).astype(bf16)


def dispatch(at, parts, residual, gain, place):
    return pl.pallas_call(
        dispatch_kernel,
        in_specs=[pl.BlockSpec(memory_space=pltpu.SMEM)] + [pl.BlockSpec(memory_space=pltpu.VMEM)] * 8,
        out_shape=(
            jax.ShapeDtypeStruct((ROWS, D), bf16),
            jax.ShapeDtypeStruct((PIECES, QUARTER), bf16),
        ),
        scratch_shapes=[pltpu.VMEM((4 * ROWS, QUARTER), bf16), pltpu.VMEM((ROWS, D), f32)],
        compiler_params=pltpu.CompilerParams(vmem_limit_bytes=VMEM_BYTES),
        cost_estimate=pl.CostEstimate(flops=120_000_000, bytes_accessed=4_000_000, transcendentals=16),
        name="dispatch",
    )(at, *parts, residual, gain, place)


def expert_kernel(x_ref, wi_ref, wo_ref, out_ref, rows_ref, both_ref, act_ref, back_ref, wi_buf, wo_buf, sems):
    copies = []
    for i in range(STEPS):
        source = wi_ref.at[pl.ds(i * DEPTH, DEPTH), :]
        copies.append(pltpu.make_async_copy(source, wi_buf.at[i], sems.at[i]))
    for i in range(4):
        source = wo_ref.at[:, pl.ds(i * QUARTER, QUARTER)]
        copies.append(pltpu.make_async_copy(source, wo_buf.at[i], sems.at[STEPS + i]))
    ahead = 6
    for i in range(ahead):
        copies[i].start()

    def arrive(i):
        copies[i].wait()
        if i + ahead < len(copies):
            copies[i + ahead].start()

    def matches(to, frm):
        same_quarter = to // 64 == frm % 8 // 2
        return (same_quarter & (to % 64 // 2 == frm // 8) & (to % 2 == frm % 2)).astype(bf16)

    sort = matches(iota((256, 256), 0), iota((256, 256), 1))
    unsort = matches(iota((256, 256), 1), iota((256, 256), 0))
    for b in range(4):
        sorted_rows = mm(sort, x_ref[b * 256 : (b + 1) * 256, :]).astype(bf16)
        for quarter in range(4):
            rows_ref[b * 64 : (b + 1) * 64, quarter * QUARTER : (quarter + 1) * QUARTER] = sorted_rows[
                quarter * 64 : (quarter + 1) * 64
            ]

    for i in range(STEPS):
        arrive(i)
        part = rows_ref[:, i * DEPTH : (i + 1) * DEPTH]
        for column in range(0, 2 * FF, 512):
            columns = slice(column, column + 512)
            more = mm(part, wi_buf[i, :, columns])
            if i < STEPS - 1:
                both_ref[:, columns] = more if i == 0 else both_ref[:, columns] + more
            elif column < FF:
                both_ref[:, columns] += more
            else:
                up = both_ref[:, columns] + more
                gates = slice(column - FF, column - FF + 512)
                act_ref[:, gates] = (jax.nn.silu(both_ref[:, gates]) * up).astype(bf16)

    for quarter in range(4):
        arrive(STEPS + quarter)
        result = mm(act_ref[...], wo_buf[quarter]).astype(bf16)
        for b in range(4):
            back_ref[b, quarter * 64 : (quarter + 1) * 64, :] = result[b * 64 : (b + 1) * 64]
    for b in range(4):
        out_ref[b * 256 : (b + 1) * 256, :] = mm(unsort, back_ref[b]).astype(bf16)


def expert(pieces, w_in, w_out):
    rows = 2 * EXPERTS
    return pl.pallas_call(
        expert_kernel,
        in_specs=[
            pl.BlockSpec(memory_space=pltpu.VMEM),
            pl.BlockSpec(memory_space=pltpu.HBM),
            pl.BlockSpec(memory_space=pltpu.HBM),
        ],
        out_specs=pl.BlockSpec(memory_space=pltpu.VMEM),
        out_shape=jax.ShapeDtypeStruct((PIECES, QUARTER), bf16),
        scratch_shapes=[
            pltpu.VMEM((rows, D), bf16),
            pltpu.VMEM((rows, 2 * FF), f32),
            pltpu.VMEM((rows, FF), bf16),
            pltpu.VMEM((4, 256, QUARTER), bf16),
            pltpu.VMEM((STEPS, DEPTH, 2 * FF), bf16),
            pltpu.VMEM((4, FF, QUARTER), bf16),
            pltpu.SemaphoreType.DMA((STEPS + 4,)),
        ],
        compiler_params=pltpu.CompilerParams(vmem_limit_bytes=48 * 1024 * 1024),
        cost_estimate=pl.CostEstimate(
            flops=2 * rows * 3 * D * FF, bytes_accessed=26_000_000, transcendentals=rows * FF
        ),
        name="expert",
    )(pieces, w_in, w_out)


def combine_kernel(back_ref, weight_ref, hidden_ref, out_ref):
    both = mm(weight_ref[...], back_ref[...])
    for quarter in range(4):
        columns = slice(quarter * QUARTER, (quarter + 1) * QUARTER)
        rows = slice(quarter * ROWS, (quarter + 1) * ROWS)
        low_rows = slice((4 + quarter) * ROWS, (5 + quarter) * ROWS)
        out_ref[:, columns] = (hidden_ref[:, columns].astype(f32) + (both[rows] + both[low_rows])).astype(bf16)


def combine(back, weight, hidden):
    return pl.pallas_call(
        combine_kernel,
        out_shape=jax.ShapeDtypeStruct((ROWS, D), bf16),
        compiler_params=pltpu.CompilerParams(vmem_limit_bytes=VMEM_BYTES),
        cost_estimate=pl.CostEstimate(flops=240_000_000, bytes_accessed=2_400_000, transcendentals=0),
        name="combine",
    )(back, weight, hidden)


def local(
    queries,
    cached_latent_rows,
    lengths,
    value_up_weight,
    out_proj,
    residual_in,
    norm_gain,
    routes,
    route_scores,
    w_gate_up,
    w_down,
):
    def along_z(block, step):
        return lax.ppermute(block, "z", [(i, (i - step) % 4) for i in range(4)])

    def other_core(block):
        return lax.ppermute(block, "core", [(0, 1), (1, 0)])

    own = out_proj.T
    at = jnp.stack([lax.axis_index(name) for name in ("z", "y", "x", "core")]).astype(jnp.int32)
    next_block, last_block = along_z(own, 1), along_z(own, 3)
    head_out = attention(
        queries.transpose(1, 2, 0),
        cached_latent_rows.transpose(1, 2, 0),
        lengths.reshape(1, REQUESTS),
        value_up_weight,
    )
    far_head = along_z(head_out, 2)
    next_block, last_block = hold(next_block, last_block, head_out)
    place, weight = plan(routes, route_scores)
    own_pair = [own, other_core(own)]
    near_pairs = own_pair + [next_block, other_core(next_block), last_block, other_core(last_block)]
    near = exchange("x", project("x", at, head_out, near_pairs))
    far = exchange("y", project("y", at, far_head, own_pair))
    far = along_z(total(exchange("x", reduce("x", at, far))), 2)
    parts = exchange("y", reduce("y", at, near)) + [far]
    hidden, outgoing = dispatch(at, parts, residual_in, norm_gain.reshape(1, D), place)
    everyone = ("z", "core", "y", "x")
    arrived = lax.all_to_all(
        outgoing.reshape(EXPERTS, 8, QUARTER), everyone, split_axis=0, concat_axis=0, tiled=True
    )
    produced = expert(arrived.reshape(PIECES, QUARTER), w_gate_up[0], w_down[0])
    returned = lax.all_to_all(
        produced.reshape(EXPERTS, 8, QUARTER), everyone, split_axis=0, concat_axis=0, tiled=True
    )
    return combine(returned.reshape(PIECES, QUARTER), weight, hidden)


def solution(mesh):
    fine = Mesh(mesh.devices.reshape(4, 2, 4, 4), ("z", "core", "y", "x"))
    dp, ex, both = ("z", "core"), ("y", "x"), ("z", "core", "y", "x")
    in_specs = (
        P(dp, ex, None),
        P(dp, None, None),
        P(dp),
        P(ex, None, None),
        P(ex, dp),
        P(both, None),
        P(),
        P(both, None),
        P(both, None),
        P(both, None, None),
        P(both, None, None),
    )
    return jax.shard_map(local, mesh=fine, in_specs=in_specs, out_specs=P(both, None), check_vma=False)
```

```python
import jax
import jax.numpy as jnp
from jax import lax
from jax.experimental import pallas as pl
from jax.experimental.pallas import tpu as pltpu
from jax.sharding import Mesh, PartitionSpec as P

D = 3584
FF = 1024
HEADS = 4
LATENT = 512
WIDTH = 576
VALUE = 128
SLOTS = 8
TOP = 8
EXPERTS = 128
ROWS = 16
REQUESTS = 256
QUARTER = D // 4
PIECES = EXPERTS * 8
COLUMNS = 448

score_scale = 0.07216878364870323

f32, bf16 = jnp.float32, jnp.bfloat16
VMEM_BYTES = 16 * 1024 * 1024


def iota(shape, dim):
    return lax.broadcasted_iota(jnp.int32, shape, dim)


def mm(a, b):
    return jnp.dot(a, b, preferred_element_type=f32)


def attention_kernel(q_ref, k_ref, len_ref, up_ref, out_ref, lat_ref):
    def score_step(i, sums):
        rows = pl.ds(i * 16, 16)
        q = [q_ref[h, rows, :].astype(f32) for h in range(HEADS)]
        k = [k_ref[s, rows, :].astype(f32) for s in range(SLOTS)]
        new = []
        for h in range(HEADS):
            for s in range(SLOTS):
                prod = q[h] * k[s]
                new.append(sums[h * SLOTS + s] + (prod[:8] + prod[8:]))
        return tuple(new)

    sums = lax.fori_loop(
        0, WIDTH // 16, score_step, tuple(jnp.zeros((8, 128), f32) for _ in range(HEADS * SLOTS))
    )
    live = iota((SLOTS, 128), 0) < len_ref[...]
    probs = []
    for h in range(HEADS):
        scores = jnp.concatenate(
            [jnp.sum(sums[h * SLOTS + s], axis=0, keepdims=True) for s in range(SLOTS)], axis=0
        )
        scores = jnp.where(live, scores * score_scale, -1e30)
        expo = jnp.exp(scores - jnp.max(scores, axis=0, keepdims=True))
        prob = (expo / jnp.sum(expo, axis=0, keepdims=True)).astype(bf16).astype(f32)
        probs.append([jnp.broadcast_to(prob[s : s + 1], (8, 128)) for s in range(SLOTS)])

    @pl.loop(0, LATENT // 16)
    def _(i):
        rows = pl.ds(i * 16, 16)
        k = [k_ref[s, rows, :].astype(f32) for s in range(SLOTS)]
        for h in range(HEADS):
            low = sum(probs[h][s] * k[s][:8] for s in range(SLOTS))
            high = sum(probs[h][s] * k[s][8:] for s in range(SLOTS))
            lat_ref[h, rows, :] = jnp.concatenate([low, high], axis=0).astype(bf16)

    for h in range(HEADS):
        out_ref[:, h * VALUE : (h + 1) * VALUE] = lax.dot_general(
            lat_ref[h], up_ref[h], (((0,), (0,)), ((), ())), preferred_element_type=f32
        ).astype(bf16)


def attention(q, k, lengths, up):
    return pl.pallas_call(
        attention_kernel,
        grid=(REQUESTS // 128,),
        in_specs=[
            pl.BlockSpec((HEADS, WIDTH, 128), lambda j: (0, 0, j)),
            pl.BlockSpec((SLOTS, WIDTH, 128), lambda j: (0, 0, j)),
            pl.BlockSpec((1, 128), lambda j: (0, j)),
            pl.BlockSpec((HEADS, LATENT, VALUE), lambda j: (0, 0, 0)),
        ],
        out_specs=pl.BlockSpec((128, HEADS * VALUE), lambda j: (j, 0)),
        out_shape=jax.ShapeDtypeStruct((REQUESTS, HEADS * VALUE), bf16),
        scratch_shapes=[pltpu.VMEM((HEADS, LATENT, 128), bf16)],
        compiler_params=pltpu.CompilerParams(vmem_limit_bytes=VMEM_BYTES),
        cost_estimate=pl.CostEstimate(flops=9_000_000_000, bytes_accessed=4_200_000, transcendentals=8192),
        name="attention",
    )(
        pltpu.with_memory_space_constraint(q, pltpu.HBM),
        pltpu.with_memory_space_constraint(k, pltpu.HBM),
        lengths,
        up,
    )


def plan_kernel(at_ref, routes_ref, score_ref, gain_ref, place_ref, weight_ref, gain_out, at_out):
    for i in range(4):
        at_out[i] = at_ref[i]
    gain_out[...] = gain_ref[...]
    routes, scores = routes_ref[...], score_ref[...]
    gates = 2.5 * scores / jnp.sum(scores, axis=0, keepdims=True)
    named = jnp.zeros((EXPERTS, ROWS), f32)
    gate = jnp.zeros((EXPERTS, ROWS), f32)
    for k in range(TOP):
        hit = iota((EXPERTS, ROWS), 0) == routes[k : k + 1, :]
        named += hit.astype(f32)
        gate += jnp.where(hit, gates[k : k + 1, :], 0.0)
    before = (iota((ROWS, ROWS), 0) < iota((ROWS, ROWS), 1)).astype(bf16)
    rank = mm(named.astype(bf16), before)

    spread = (iota((ROWS, 4 * ROWS), 1) % ROWS == iota((ROWS, 4 * ROWS), 0)).astype(bf16)
    expand = (iota((PIECES, EXPERTS), 0) // 8 == iota((PIECES, EXPERTS), 1)).astype(bf16)
    both = []
    for slot in range(2):
        here = jnp.where(rank == slot, named, 0.0).astype(bf16)
        both.append(mm(expand, mm(here, spread).astype(bf16)))
    n = iota((PIECES, 4 * ROWS), 0)
    place = jnp.where(n % 2 == 0, both[0], both[1])
    place_ref[...] = jnp.where(n % 8 // 2 == iota((PIECES, 4 * ROWS), 1) // ROWS, place, 0.0).astype(bf16)

    expand = (iota((EXPERTS, PIECES), 1) // 8 == iota((EXPERTS, PIECES), 0)).astype(bf16)
    n = iota((ROWS, PIECES), 1)
    high, low = [], []
    for slot in range(2):
        part = jnp.where(rank == slot, gate, 0.0).T
        top = part.astype(bf16)
        high.append(mm(top, expand))
        low.append(mm((part - top.astype(f32)).astype(bf16), expand))
    for i, parts in enumerate((high, low)):
        row = jnp.where(n % 2 == 0, parts[0], parts[1])
        for quarter in range(4):
            weight_ref[pl.ds((i * 4 + quarter) * ROWS, ROWS), :] = jnp.where(
                n % 8 // 2 == quarter, row, 0.0
            ).astype(bf16)


def plan(at, routes, scores, gain):
    return pl.pallas_call(
        plan_kernel,
        out_shape=(
            jax.ShapeDtypeStruct((PIECES, 4 * ROWS), bf16),
            jax.ShapeDtypeStruct((8 * ROWS, PIECES), bf16),
            jax.ShapeDtypeStruct((1, D), f32),
            jax.ShapeDtypeStruct((4,), jnp.int32),
        ),
        in_specs=[pl.BlockSpec(memory_space=pltpu.SMEM)] + [pl.BlockSpec(memory_space=pltpu.VMEM)] * 3,
        out_specs=[pl.BlockSpec(memory_space=pltpu.VMEM)] * 3 + [pl.BlockSpec(memory_space=pltpu.SMEM)],
        compiler_params=pltpu.CompilerParams(vmem_limit_bytes=VMEM_BYTES),
        cost_estimate=pl.CostEstimate(flops=60_000_000, bytes_accessed=500_000, transcendentals=0),
        name="plan",
    )(at, routes.T, scores.T, gain)


def fetch_kernel(at_ref, wi_ref, wo_ref, wi_out, wo_out, at_out, sems):
    copies = (
        pltpu.make_async_copy(wi_ref, wi_out, sems.at[0]),
        pltpu.make_async_copy(wo_ref, wo_out, sems.at[1]),
    )
    for copy in copies:
        copy.start()
    for i in range(4):
        at_out[i] = at_ref[i]
    for copy in copies:
        copy.wait()


def fetch(at, w_in, w_out):
    return pl.pallas_call(
        fetch_kernel,
        in_specs=[pl.BlockSpec(memory_space=pltpu.SMEM)] + [pl.BlockSpec(memory_space=pltpu.HBM)] * 2,
        out_specs=[pl.BlockSpec(memory_space=pltpu.VMEM)] * 2 + [pl.BlockSpec(memory_space=pltpu.SMEM)],
        out_shape=[
            pltpu.VMEM(w_in.shape, bf16),
            pltpu.VMEM(w_out.shape, bf16),
            jax.ShapeDtypeStruct((4,), jnp.int32),
        ],
        scratch_shapes=[pltpu.SemaphoreType.DMA((2,))],
        compiler_params=pltpu.CompilerParams(vmem_limit_bytes=VMEM_BYTES),
        cost_estimate=pl.CostEstimate(flops=0, bytes_accessed=26_000_000, transcendentals=0),
        name="fetch",
    )(at, pltpu.with_memory_space_constraint(w_in, pltpu.HBM), pltpu.with_memory_space_constraint(w_out, pltpu.HBM))


def project_kernel(at_ref, head_ref, other_ref, *refs):
    blocks, out_ref, (rows_ref, w_ref) = refs[:4], refs[4], refs[5:]
    for i in range(REQUESTS // ROWS):
        rows = slice(i * ROWS, (i + 1) * ROWS)
        rows_ref[2 * i * ROWS : (2 * i + 1) * ROWS, :] = head_ref[rows, :]
        rows_ref[(2 * i + 1) * ROWS : (2 * i + 2) * ROWS, :] = other_ref[rows, :]
    for i in range(4):
        w_ref[i * COLUMNS : (i + 1) * COLUMNS, :] = blocks[i][...]
    for i in range(2):
        columns = slice(i * 2 * COLUMNS, (i + 1) * 2 * COLUMNS)
        out_ref[:, columns] = lax.dot_general(
            rows_ref[...], w_ref[columns, :], (((1,), (1,)), ((), ())), preferred_element_type=f32
        ).astype(bf16)


def project(at, head_out, other_head, blocks):
    return pl.pallas_call(
        project_kernel,
        in_specs=[pl.BlockSpec(memory_space=pltpu.SMEM)] + [pl.BlockSpec(memory_space=pltpu.VMEM)] * 6,
        out_specs=pl.BlockSpec(memory_space=pltpu.VMEM),
        out_shape=jax.ShapeDtypeStruct((2 * REQUESTS, 4 * COLUMNS), bf16),
        scratch_shapes=[
            pltpu.VMEM((2 * REQUESTS, HEADS * VALUE), bf16),
            pltpu.VMEM((4 * COLUMNS, HEADS * VALUE), bf16),
        ],
        compiler_params=pltpu.CompilerParams(vmem_limit_bytes=VMEM_BYTES),
        cost_estimate=pl.CostEstimate(flops=2 * REQUESTS * 512 * D, bytes_accessed=4_500_000, transcendentals=0),
        name="project",
    )(at, head_out, other_head, *blocks)


def total_kernel(parts_ref, own_ref, other_ref):
    for out_ref, start in ((own_ref, 0), (other_ref, ROWS)):
        rows = slice(start, start + ROWS)
        total = parts_ref[0, rows, :].astype(f32)
        for i in range(1, parts_ref.shape[0]):
            total += parts_ref[i, rows, :].astype(f32)
        out_ref[...] = total.astype(bf16)


def total(parts):
    return pl.pallas_call(
        total_kernel,
        out_shape=[jax.ShapeDtypeStruct((ROWS, 4 * COLUMNS), bf16)] * 2,
        compiler_params=pltpu.CompilerParams(vmem_limit_bytes=VMEM_BYTES),
        cost_estimate=pl.CostEstimate(flops=1_000_000, bytes_accessed=2_000_000, transcendentals=0),
        name="total",
    )(parts)


def dispatch_kernel(
    at_ref, own_ref, other_ref, res_ref, gain_ref, place_ref, hidden_ref, out_ref, norm_ref, sum_ref
):
    z, core = at_ref[0], at_ref[3]
    own, other = own_ref[...].astype(f32), other_ref[...].astype(f32)
    even = jnp.where(core == 0, own, other)
    odd = jnp.where(core == 0, other, own)
    for step in range(4):
        columns = slice(step * COLUMNS, (step + 1) * COLUMNS)
        start = pl.multiple_of(lax.rem(z + step, 4) * QUARTER, 128)
        sum_ref[:, pl.ds(start, QUARTER)] = jnp.concatenate([even[:, columns], odd[:, columns]], axis=1)
    hidden = (res_ref[...].astype(f32) + sum_ref[...]).astype(bf16)
    hidden_ref[...] = hidden
    hidden = hidden.astype(f32)
    inverse = lax.rsqrt(jnp.mean(hidden * hidden, axis=1, keepdims=True) + 1e-6)
    normed = (hidden * inverse * gain_ref[...]).astype(bf16)
    for quarter in range(4):
        norm_ref[pl.ds(quarter * ROWS, ROWS), :] = normed[:, quarter * QUARTER : (quarter + 1) * QUARTER]

    @pl.loop(0, 4)
    def _(i):
        rows = pl.ds(i * (PIECES // 4), PIECES // 4)
        out_ref[rows, :] = mm(place_ref[rows, :], norm_ref[...]).astype(bf16)


def dispatch(at, own, other, residual, gain, place):
    return pl.pallas_call(
        dispatch_kernel,
        in_specs=[pl.BlockSpec(memory_space=pltpu.SMEM)] + [pl.BlockSpec(memory_space=pltpu.VMEM)] * 5,
        out_shape=(
            jax.ShapeDtypeStruct((ROWS, D), bf16),
            jax.ShapeDtypeStruct((PIECES, QUARTER), bf16),
        ),
        scratch_shapes=[pltpu.VMEM((4 * ROWS, QUARTER), bf16), pltpu.VMEM((ROWS, D), f32)],
        compiler_params=pltpu.CompilerParams(vmem_limit_bytes=VMEM_BYTES),
        cost_estimate=pl.CostEstimate(flops=120_000_000, bytes_accessed=4_000_000, transcendentals=16),
        name="dispatch",
    )(at, own, other, residual, gain, place)


def expert_kernel(x_ref, wi_ref, wo_ref, out_ref, rows_ref, act_ref, back_ref):
    half = FF // 4

    def matches(to, frm):
        same_quarter = to // 64 == frm % 8 // 2
        return (same_quarter & (to % 64 // 2 == frm // 8) & (to % 2 == frm % 2)).astype(bf16)

    sort = matches(iota((256, 256), 0), iota((256, 256), 1))
    unsort = matches(iota((256, 256), 1), iota((256, 256), 0))
    for b in range(4):
        sorted_rows = mm(sort, x_ref[b * 256 : (b + 1) * 256, :]).astype(bf16)
        for quarter in range(4):
            rows_ref[b * 64 : (b + 1) * 64, quarter * QUARTER : (quarter + 1) * QUARTER] = sorted_rows[
                quarter * 64 : (quarter + 1) * 64
            ]

    for i in range(4):
        gate = mm(rows_ref[...], wi_ref[:, i * half : (i + 1) * half])
        up = mm(rows_ref[...], wi_ref[:, FF + i * half : FF + (i + 1) * half])
        act_ref[:, i * half : (i + 1) * half] = (jax.nn.silu(gate) * up).astype(bf16)

    for quarter in range(4):
        result = mm(act_ref[...], wo_ref[:, quarter * QUARTER : (quarter + 1) * QUARTER]).astype(bf16)
        for b in range(4):
            back_ref[b, quarter * 64 : (quarter + 1) * 64, :] = result[b * 64 : (b + 1) * 64]
    for b in range(4):
        out_ref[b * 256 : (b + 1) * 256, :] = mm(unsort, back_ref[b]).astype(bf16)


def expert(pieces, w_in, w_out):
    rows = 2 * EXPERTS
    return pl.pallas_call(
        expert_kernel,
        in_specs=[pl.BlockSpec(memory_space=pltpu.VMEM)] * 3,
        out_specs=pl.BlockSpec(memory_space=pltpu.VMEM),
        out_shape=jax.ShapeDtypeStruct((PIECES, QUARTER), bf16),
        scratch_shapes=[
            pltpu.VMEM((rows, D), bf16),
            pltpu.VMEM((rows, FF), bf16),
            pltpu.VMEM((4, 256, QUARTER), bf16),
        ],
        compiler_params=pltpu.CompilerParams(vmem_limit_bytes=VMEM_BYTES),
        cost_estimate=pl.CostEstimate(
            flops=2 * rows * 3 * D * FF, bytes_accessed=26_000_000, transcendentals=rows * FF
        ),
        name="expert",
    )(
        pieces,
        w_in,
        w_out,
    )


def combine_kernel(back_ref, weight_ref, hidden_ref, out_ref):
    both = mm(weight_ref[...], back_ref[...])
    for quarter in range(4):
        columns = slice(quarter * QUARTER, (quarter + 1) * QUARTER)
        rows = slice(quarter * ROWS, (quarter + 1) * ROWS)
        low_rows = slice((4 + quarter) * ROWS, (5 + quarter) * ROWS)
        out_ref[:, columns] = (hidden_ref[:, columns].astype(f32) + (both[rows] + both[low_rows])).astype(bf16)


def combine(back, weight, hidden):
    return pl.pallas_call(
        combine_kernel,
        out_shape=jax.ShapeDtypeStruct((ROWS, D), bf16),
        compiler_params=pltpu.CompilerParams(vmem_limit_bytes=VMEM_BYTES),
        cost_estimate=pl.CostEstimate(flops=240_000_000, bytes_accessed=2_400_000, transcendentals=0),
        name="combine",
    )(back, weight, hidden)


def local(
    queries,
    cached_latent_rows,
    lengths,
    value_up_weight,
    out_proj,
    residual_in,
    norm_gain,
    routes,
    route_scores,
    w_gate_up,
    w_down,
):
    own = out_proj.T
    others = [lax.ppermute(own, "z", [(i, (i - step) % 4) for i in range(4)]) for step in (1, 2, 3)]
    at = jnp.stack([lax.axis_index(name) for name in ("z", "y", "x", "core")]).astype(jnp.int32)

    def other_core(block):
        return lax.ppermute(block, "core", [(0, 1), (1, 0)])

    head_out = attention(
        queries.transpose(1, 2, 0),
        cached_latent_rows.transpose(1, 2, 0),
        lengths.reshape(1, REQUESTS),
        value_up_weight,
    )
    place, weight, gain, at = plan(at, routes, route_scores, norm_gain.reshape(1, D))
    w_in, w_out, at = fetch(at, w_gate_up[0], w_down[0])
    shares = project(at, head_out, other_core(head_out), (own, *others))
    parts = lax.all_to_all(
        shares.reshape(16, 2 * ROWS, 4 * COLUMNS), ("y", "x"), split_axis=0, concat_axis=0, tiled=True
    )
    own_total, other_total = total(parts)
    hidden, outgoing = dispatch(at, own_total, other_core(other_total), residual_in, gain, place)
    everyone = ("z", "core", "y", "x")
    arrived = lax.all_to_all(
        outgoing.reshape(EXPERTS, 8, QUARTER), everyone, split_axis=0, concat_axis=0, tiled=True
    )
    produced = expert(arrived.reshape(PIECES, QUARTER), w_in, w_out)
    returned = lax.all_to_all(
        produced.reshape(EXPERTS, 8, QUARTER), everyone, split_axis=0, concat_axis=0, tiled=True
    )
    return combine(returned.reshape(PIECES, QUARTER), weight, hidden)


def solution(mesh):
    fine = Mesh(mesh.devices.reshape(4, 2, 4, 4), ("z", "core", "y", "x"))
    dp, ex, both = ("z", "core"), ("y", "x"), ("z", "core", "y", "x")
    in_specs = (
        P(dp, ex, None),
        P(dp, None, None),
        P(dp),
        P(ex, None, None),
        P(ex, dp),
        P(both, None),
        P(),
        P(both, None),
        P(both, None),
        P(both, None, None),
        P(both, None, None),
    )
    return jax.shard_map(local, mesh=fine, in_specs=in_specs, out_specs=P(both, None), check_vma=False)
```

```python
import jax
import jax.numpy as jnp
from jax import lax
from jax.experimental import pallas as pl
from jax.experimental.pallas import tpu as pltpu
from jax.sharding import Mesh, PartitionSpec as P

D = 3584
FF = 1024
HEADS = 4
LATENT = 512
WIDTH = 576
VALUE = 128
SLOTS = 8
TOP = 8
EXPERTS = 128
ROWS = 16
REQUESTS = 256
QUARTER = D // 4
PIECES = EXPERTS * 8
COLUMNS = 448
CHIPS = (0, 2, 1, 3)

score_scale = 0.07216878364870323

f32, bf16 = jnp.float32, jnp.bfloat16
VMEM_BYTES = 16 * 1024 * 1024


def iota(shape, dim):
    return lax.broadcasted_iota(jnp.int32, shape, dim)


def mm(a, b):
    return jnp.dot(a, b, preferred_element_type=f32)


def attention_kernel(q_ref, k_ref, len_ref, up_ref, out_ref, lat_ref):
    def score_step(i, sums):
        rows = pl.ds(i * 16, 16)
        q = [q_ref[h, rows, :].astype(f32) for h in range(HEADS)]
        k = [k_ref[s, rows, :].astype(f32) for s in range(SLOTS)]
        new = []
        for h in range(HEADS):
            for s in range(SLOTS):
                prod = q[h] * k[s]
                new.append(sums[h * SLOTS + s] + (prod[:8] + prod[8:]))
        return tuple(new)

    sums = lax.fori_loop(
        0, WIDTH // 16, score_step, tuple(jnp.zeros((8, 128), f32) for _ in range(HEADS * SLOTS))
    )
    live = iota((SLOTS, 128), 0) < len_ref[...]
    probs = []
    for h in range(HEADS):
        scores = jnp.concatenate(
            [jnp.sum(sums[h * SLOTS + s], axis=0, keepdims=True) for s in range(SLOTS)], axis=0
        )
        scores = jnp.where(live, scores * score_scale, -1e30)
        expo = jnp.exp(scores - jnp.max(scores, axis=0, keepdims=True))
        prob = (expo / jnp.sum(expo, axis=0, keepdims=True)).astype(bf16).astype(f32)
        probs.append([jnp.broadcast_to(prob[s : s + 1], (8, 128)) for s in range(SLOTS)])

    @pl.loop(0, LATENT // 16)
    def _(i):
        rows = pl.ds(i * 16, 16)
        k = [k_ref[s, rows, :].astype(f32) for s in range(SLOTS)]
        for h in range(HEADS):
            low = sum(probs[h][s] * k[s][:8] for s in range(SLOTS))
            high = sum(probs[h][s] * k[s][8:] for s in range(SLOTS))
            lat_ref[h, rows, :] = jnp.concatenate([low, high], axis=0).astype(bf16)

    for h in range(HEADS):
        out_ref[:, h * VALUE : (h + 1) * VALUE] = lax.dot_general(
            lat_ref[h], up_ref[h], (((0,), (0,)), ((), ())), preferred_element_type=f32
        ).astype(bf16)


def attention(q, k, lengths, up):
    return pl.pallas_call(
        attention_kernel,
        grid=(REQUESTS // 128,),
        in_specs=[
            pl.BlockSpec((HEADS, WIDTH, 128), lambda j: (0, 0, j)),
            pl.BlockSpec((SLOTS, WIDTH, 128), lambda j: (0, 0, j)),
            pl.BlockSpec((1, 128), lambda j: (0, j)),
            pl.BlockSpec((HEADS, LATENT, VALUE), lambda j: (0, 0, 0)),
        ],
        out_specs=pl.BlockSpec((128, HEADS * VALUE), lambda j: (j, 0)),
        out_shape=jax.ShapeDtypeStruct((REQUESTS, HEADS * VALUE), bf16),
        scratch_shapes=[pltpu.VMEM((HEADS, LATENT, 128), bf16)],
        compiler_params=pltpu.CompilerParams(vmem_limit_bytes=VMEM_BYTES),
        cost_estimate=pl.CostEstimate(flops=9_000_000_000, bytes_accessed=4_200_000, transcendentals=8192),
        name="attention",
    )(
        pltpu.with_memory_space_constraint(q, pltpu.HBM),
        pltpu.with_memory_space_constraint(k, pltpu.HBM),
        lengths,
        up,
    )


def plan_kernel(routes_ref, score_ref, place_ref, weight_ref):
    routes, scores = routes_ref[...], score_ref[...]
    gates = 2.5 * scores / jnp.sum(scores, axis=0, keepdims=True)
    named = jnp.zeros((EXPERTS, ROWS), f32)
    gate = jnp.zeros((EXPERTS, ROWS), f32)
    for k in range(TOP):
        hit = iota((EXPERTS, ROWS), 0) == routes[k : k + 1, :]
        named += hit.astype(f32)
        gate += jnp.where(hit, gates[k : k + 1, :], 0.0)
    before = (iota((ROWS, ROWS), 0) < iota((ROWS, ROWS), 1)).astype(bf16)
    rank = mm(named.astype(bf16), before)

    spread = (iota((ROWS, 4 * ROWS), 1) % ROWS == iota((ROWS, 4 * ROWS), 0)).astype(bf16)
    expand = (iota((PIECES, EXPERTS), 0) // 8 == iota((PIECES, EXPERTS), 1)).astype(bf16)
    both = []
    for slot in range(2):
        here = jnp.where(rank == slot, named, 0.0).astype(bf16)
        both.append(mm(expand, mm(here, spread).astype(bf16)))
    n = iota((PIECES, 4 * ROWS), 0)
    place = jnp.where(n % 2 == 0, both[0], both[1])
    place_ref[...] = jnp.where(n % 8 // 2 == iota((PIECES, 4 * ROWS), 1) // ROWS, place, 0.0).astype(bf16)

    expand = (iota((EXPERTS, PIECES), 1) // 8 == iota((EXPERTS, PIECES), 0)).astype(bf16)
    n = iota((ROWS, PIECES), 1)
    high, low = [], []
    for slot in range(2):
        part = jnp.where(rank == slot, gate, 0.0).T
        top = part.astype(bf16)
        high.append(mm(top, expand))
        low.append(mm((part - top.astype(f32)).astype(bf16), expand))
    for i, parts in enumerate((high, low)):
        row = jnp.where(n % 2 == 0, parts[0], parts[1])
        for quarter in range(4):
            weight_ref[pl.ds((i * 4 + quarter) * ROWS, ROWS), :] = jnp.where(
                n % 8 // 2 == quarter, row, 0.0
            ).astype(bf16)


def plan(routes, scores):
    return pl.pallas_call(
        plan_kernel,
        out_shape=(
            jax.ShapeDtypeStruct((PIECES, 4 * ROWS), bf16),
            jax.ShapeDtypeStruct((8 * ROWS, PIECES), bf16),
        ),
        compiler_params=pltpu.CompilerParams(vmem_limit_bytes=VMEM_BYTES),
        cost_estimate=pl.CostEstimate(flops=60_000_000, bytes_accessed=500_000, transcendentals=0),
        name="plan",
    )(routes.T, scores.T)


def fetch_kernel(gain_ref, wi_ref, wo_ref, wi_out, wo_out, gain_out, sems):
    gain_out[...] = gain_ref[...]
    copies = []
    for source, target, pieces in ((wi_ref, wi_out, 8), (wo_ref, wo_out, 4)):
        depth = source.shape[0] // pieces
        for i in range(pieces):
            rows = pl.ds(i * depth, depth)
            copies.append(pltpu.make_async_copy(source.at[rows, :], target.at[rows, :], sems.at[len(copies)]))
    for copy in copies:
        copy.start()
    for copy in copies:
        copy.wait()


def fetch(gain, w_in, w_out):
    in_hbm = [pltpu.with_memory_space_constraint(w, pltpu.HBM) for w in (w_in, w_out)]
    return pl.pallas_call(
        fetch_kernel,
        in_specs=[pl.BlockSpec(memory_space=space) for space in (pltpu.VMEM, pltpu.HBM, pltpu.HBM)],
        out_specs=[pl.BlockSpec(memory_space=pltpu.VMEM)] * 3,
        out_shape=[
            pltpu.VMEM(w_in.shape, bf16),
            pltpu.VMEM(w_out.shape, bf16),
            jax.ShapeDtypeStruct((1, D), f32),
        ],
        scratch_shapes=[pltpu.SemaphoreType.DMA((12,))],
        compiler_params=pltpu.CompilerParams(vmem_limit_bytes=VMEM_BYTES),
        cost_estimate=pl.CostEstimate(flops=0, bytes_accessed=26_000_000, transcendentals=0),
        name="fetch",
    )(gain, *in_hbm)


def project_kernel(head_ref, other_ref, *refs):
    blocks, out_ref, (rows_ref, w_ref) = refs[:4], refs[6], refs[7:]
    for i in range(REQUESTS // ROWS):
        rows = slice(i * ROWS, (i + 1) * ROWS)
        rows_ref[2 * i * ROWS : (2 * i + 1) * ROWS, :] = head_ref[rows, :]
        rows_ref[(2 * i + 1) * ROWS : (2 * i + 2) * ROWS, :] = other_ref[rows, :]
    for i in range(4):
        w_ref[i * COLUMNS : (i + 1) * COLUMNS, :] = blocks[i][...]
    for i in range(2):
        columns = slice(i * 2 * COLUMNS, (i + 1) * 2 * COLUMNS)
        out_ref[:, columns] = lax.dot_general(
            rows_ref[...], w_ref[columns, :], (((1,), (1,)), ((), ())), preferred_element_type=f32
        ).astype(bf16)


def project(head_out, other_head, blocks, place, gain):
    return pl.pallas_call(
        project_kernel,
        in_specs=[pl.BlockSpec(memory_space=pltpu.VMEM)] * 8,
        out_specs=pl.BlockSpec(memory_space=pltpu.VMEM),
        out_shape=jax.ShapeDtypeStruct((2 * REQUESTS, 4 * COLUMNS), bf16),
        scratch_shapes=[
            pltpu.VMEM((2 * REQUESTS, HEADS * VALUE), bf16),
            pltpu.VMEM((4 * COLUMNS, HEADS * VALUE), bf16),
        ],
        compiler_params=pltpu.CompilerParams(vmem_limit_bytes=VMEM_BYTES),
        cost_estimate=pl.CostEstimate(flops=2 * REQUESTS * 512 * D, bytes_accessed=4_500_000, transcendentals=0),
        name="project",
    )(head_out, other_head, *blocks, place, gain)


def total_kernel(parts_ref, own_ref, other_ref):
    for out_ref, start in ((own_ref, 0), (other_ref, ROWS)):
        rows = slice(start, start + ROWS)
        total = parts_ref[0, rows, :].astype(f32)
        for i in range(1, parts_ref.shape[0]):
            total += parts_ref[i, rows, :].astype(f32)
        out_ref[...] = total.astype(bf16)


def total(parts):
    return pl.pallas_call(
        total_kernel,
        out_shape=[jax.ShapeDtypeStruct((ROWS, 4 * COLUMNS), bf16)] * 2,
        compiler_params=pltpu.CompilerParams(vmem_limit_bytes=VMEM_BYTES),
        cost_estimate=pl.CostEstimate(flops=1_000_000, bytes_accessed=2_000_000, transcendentals=0),
        name="total",
    )(parts)


def dispatch_kernel(own_ref, other_ref, res_ref, gain_ref, place_ref, hidden_ref, out_ref, norm_ref, sum_ref):
    z, core = lax.axis_index("z"), lax.axis_index("core")
    own, other = own_ref[...].astype(f32), other_ref[...].astype(f32)
    even = jnp.where(core == 0, own, other)
    odd = jnp.where(core == 0, other, own)
    for i, step in enumerate(CHIPS):
        columns = slice(i * COLUMNS, (i + 1) * COLUMNS)
        start = pl.multiple_of(lax.rem(z + step, 4) * QUARTER, 128)
        sum_ref[:, pl.ds(start, QUARTER)] = jnp.concatenate([even[:, columns], odd[:, columns]], axis=1)
    hidden = (res_ref[...].astype(f32) + sum_ref[...]).astype(bf16)
    hidden_ref[...] = hidden
    hidden = hidden.astype(f32)
    inverse = lax.rsqrt(jnp.mean(hidden * hidden, axis=1, keepdims=True) + 1e-6)
    normed = (hidden * inverse * gain_ref[...]).astype(bf16)
    for quarter in range(4):
        norm_ref[pl.ds(quarter * ROWS, ROWS), :] = normed[:, quarter * QUARTER : (quarter + 1) * QUARTER]

    @pl.loop(0, 4)
    def _(i):
        rows = pl.ds(i * (PIECES // 4), PIECES // 4)
        out_ref[rows, :] = mm(place_ref[rows, :], norm_ref[...]).astype(bf16)


def dispatch(own, other, residual, gain, place):
    return pl.pallas_call(
        dispatch_kernel,
        out_shape=(
            jax.ShapeDtypeStruct((ROWS, D), bf16),
            jax.ShapeDtypeStruct((PIECES, QUARTER), bf16),
        ),
        scratch_shapes=[pltpu.VMEM((4 * ROWS, QUARTER), bf16), pltpu.VMEM((ROWS, D), f32)],
        compiler_params=pltpu.CompilerParams(vmem_limit_bytes=VMEM_BYTES),
        cost_estimate=pl.CostEstimate(flops=120_000_000, bytes_accessed=4_000_000, transcendentals=16),
        name="dispatch",
    )(own, other, residual, gain, place)


def expert_kernel(x_ref, wi_ref, wo_ref, out_ref, rows_ref, act_ref, back_ref):
    half = FF // 4

    def matches(to, frm):
        same_quarter = to // 64 == frm % 8 // 2
        return (same_quarter & (to % 64 // 2 == frm // 8) & (to % 2 == frm % 2)).astype(bf16)

    sort = matches(iota((256, 256), 0), iota((256, 256), 1))
    unsort = matches(iota((256, 256), 1), iota((256, 256), 0))
    for b in range(4):
        sorted_rows = mm(sort, x_ref[b * 256 : (b + 1) * 256, :]).astype(bf16)
        for quarter in range(4):
            rows_ref[b * 64 : (b + 1) * 64, quarter * QUARTER : (quarter + 1) * QUARTER] = sorted_rows[
                quarter * 64 : (quarter + 1) * 64
            ]

    for i in range(4):
        gate = mm(rows_ref[...], wi_ref[:, i * half : (i + 1) * half])
        up = mm(rows_ref[...], wi_ref[:, FF + i * half : FF + (i + 1) * half])
        act_ref[:, i * half : (i + 1) * half] = (jax.nn.silu(gate) * up).astype(bf16)

    for quarter in range(4):
        result = mm(act_ref[...], wo_ref[:, quarter * QUARTER : (quarter + 1) * QUARTER]).astype(bf16)
        for b in range(4):
            back_ref[b, quarter * 64 : (quarter + 1) * 64, :] = result[b * 64 : (b + 1) * 64]
    for b in range(4):
        out_ref[b * 256 : (b + 1) * 256, :] = mm(unsort, back_ref[b]).astype(bf16)


def expert(pieces, w_in, w_out):
    rows = 2 * EXPERTS
    return pl.pallas_call(
        expert_kernel,
        in_specs=[pl.BlockSpec(memory_space=pltpu.VMEM)] * 3,
        out_specs=pl.BlockSpec(memory_space=pltpu.VMEM),
        out_shape=jax.ShapeDtypeStruct((PIECES, QUARTER), bf16),
        scratch_shapes=[
            pltpu.VMEM((rows, D), bf16),
            pltpu.VMEM((rows, FF), bf16),
            pltpu.VMEM((4, 256, QUARTER), bf16),
        ],
        compiler_params=pltpu.CompilerParams(vmem_limit_bytes=VMEM_BYTES),
        cost_estimate=pl.CostEstimate(
            flops=2 * rows * 3 * D * FF, bytes_accessed=26_000_000, transcendentals=rows * FF
        ),
        name="expert",
    )(
        pieces,
        w_in,
        w_out,
    )


def combine_kernel(back_ref, weight_ref, hidden_ref, out_ref):
    both = mm(weight_ref[...], back_ref[...])
    for quarter in range(4):
        columns = slice(quarter * QUARTER, (quarter + 1) * QUARTER)
        rows = slice(quarter * ROWS, (quarter + 1) * ROWS)
        low_rows = slice((4 + quarter) * ROWS, (5 + quarter) * ROWS)
        out_ref[:, columns] = (hidden_ref[:, columns].astype(f32) + (both[rows] + both[low_rows])).astype(bf16)


def combine(back, weight, hidden):
    return pl.pallas_call(
        combine_kernel,
        out_shape=jax.ShapeDtypeStruct((ROWS, D), bf16),
        compiler_params=pltpu.CompilerParams(vmem_limit_bytes=VMEM_BYTES),
        cost_estimate=pl.CostEstimate(flops=240_000_000, bytes_accessed=2_400_000, transcendentals=0),
        name="combine",
    )(back, weight, hidden)


def local(
    queries,
    cached_latent_rows,
    lengths,
    value_up_weight,
    out_proj,
    residual_in,
    norm_gain,
    routes,
    route_scores,
    w_gate_up,
    w_down,
):
    own = out_proj.T
    others = [lax.ppermute(own, "z", [(i, (i - step) % 4) for i in range(4)]) for step in CHIPS[1:]]
    def other_core(block):
        return lax.ppermute(block, "core", [(0, 1), (1, 0)])

    head_out = attention(
        queries.transpose(1, 2, 0),
        cached_latent_rows.transpose(1, 2, 0),
        lengths.reshape(1, REQUESTS),
        value_up_weight,
    )
    place, weight = plan(routes, route_scores)
    w_in, w_out, gain = fetch(norm_gain.reshape(1, D), w_gate_up[0], w_down[0])
    shares = project(head_out, other_core(head_out), (own, *others), place, gain)
    parts = lax.all_to_all(
        shares.reshape(16, 2 * ROWS, 4 * COLUMNS), ("y", "x"), split_axis=0, concat_axis=0, tiled=True
    )
    own_total, other_total = total(parts)
    hidden, outgoing = dispatch(own_total, other_core(other_total), residual_in, gain, place)
    everyone = ("z", "core", "y", "x")
    arrived = lax.all_to_all(
        outgoing.reshape(EXPERTS, 8, QUARTER), everyone, split_axis=0, concat_axis=0, tiled=True
    )
    produced = expert(arrived.reshape(PIECES, QUARTER), w_in, w_out)
    returned = lax.all_to_all(
        produced.reshape(EXPERTS, 8, QUARTER), everyone, split_axis=0, concat_axis=0, tiled=True
    )
    return combine(returned.reshape(PIECES, QUARTER), weight, hidden)


def solution(mesh):
    fine = Mesh(mesh.devices.reshape(4, 2, 4, 4), ("z", "core", "y", "x"))
    dp, ex, both = ("z", "core"), ("y", "x"), ("z", "core", "y", "x")
    in_specs = (
        P(dp, ex, None),
        P(dp, None, None),
        P(dp),
        P(ex, None, None),
        P(ex, dp),
        P(both, None),
        P(),
        P(both, None),
        P(both, None),
        P(both, None, None),
        P(both, None, None),
    )
    return jax.shard_map(local, mesh=fine, in_specs=in_specs, out_specs=P(both, None), check_vma=False)
```

```python
import jax
import jax.numpy as jnp
from jax import lax
from jax.experimental import pallas as pl
from jax.experimental.pallas import tpu as pltpu
from jax.sharding import Mesh, PartitionSpec as P

D = 3584
FF = 1024
HEADS = 4
LATENT = 512
WIDTH = 576
VALUE = 128
SLOTS = 8
TOP = 8
EXPERTS = 128
ROWS = 16
REQUESTS = 256
QUARTER = D // 4
PIECES = EXPERTS * 8
COLUMNS = 448
CHIPS = (0, 2, 1, 3)

score_scale = 0.07216878364870323

f32, bf16 = jnp.float32, jnp.bfloat16
VMEM_BYTES = 16 * 1024 * 1024


def iota(shape, dim):
    return lax.broadcasted_iota(jnp.int32, shape, dim)


def mm(a, b):
    return jnp.dot(a, b, preferred_element_type=f32)


def attention_kernel(q_ref, k_ref, len_ref, up_ref, out_ref, lat_ref):
    def score_step(i, sums):
        rows = pl.ds(i * 16, 16)
        q = [q_ref[h, rows, :].astype(f32) for h in range(HEADS)]
        k = [k_ref[s, rows, :].astype(f32) for s in range(SLOTS)]
        new = []
        for h in range(HEADS):
            for s in range(SLOTS):
                prod = q[h] * k[s]
                new.append(sums[h * SLOTS + s] + (prod[:8] + prod[8:]))
        return tuple(new)

    sums = lax.fori_loop(
        0, WIDTH // 16, score_step, tuple(jnp.zeros((8, 128), f32) for _ in range(HEADS * SLOTS))
    )
    live = iota((SLOTS, 128), 0) < len_ref[...]
    probs = []
    for h in range(HEADS):
        scores = jnp.concatenate(
            [jnp.sum(sums[h * SLOTS + s], axis=0, keepdims=True) for s in range(SLOTS)], axis=0
        )
        scores = jnp.where(live, scores * score_scale, -1e30)
        expo = jnp.exp(scores - jnp.max(scores, axis=0, keepdims=True))
        prob = (expo / jnp.sum(expo, axis=0, keepdims=True)).astype(bf16).astype(f32)
        probs.append([jnp.broadcast_to(prob[s : s + 1], (8, 128)) for s in range(SLOTS)])

    @pl.loop(0, LATENT // 16)
    def _(i):
        rows = pl.ds(i * 16, 16)
        k = [k_ref[s, rows, :].astype(f32) for s in range(SLOTS)]
        for h in range(HEADS):
            low = sum(probs[h][s] * k[s][:8] for s in range(SLOTS))
            high = sum(probs[h][s] * k[s][8:] for s in range(SLOTS))
            lat_ref[h, rows, :] = jnp.concatenate([low, high], axis=0).astype(bf16)

    for h in range(HEADS):
        out_ref[:, h * VALUE : (h + 1) * VALUE] = lax.dot_general(
            lat_ref[h], up_ref[h], (((0,), (0,)), ((), ())), preferred_element_type=f32
        ).astype(bf16)


def attention(q, k, lengths, up):
    return pl.pallas_call(
        attention_kernel,
        grid=(REQUESTS // 128,),
        in_specs=[
            pl.BlockSpec((HEADS, WIDTH, 128), lambda j: (0, 0, j)),
            pl.BlockSpec((SLOTS, WIDTH, 128), lambda j: (0, 0, j)),
            pl.BlockSpec((1, 128), lambda j: (0, j)),
            pl.BlockSpec((HEADS, LATENT, VALUE), lambda j: (0, 0, 0)),
        ],
        out_specs=pl.BlockSpec((128, HEADS * VALUE), lambda j: (j, 0)),
        out_shape=jax.ShapeDtypeStruct((REQUESTS, HEADS * VALUE), bf16),
        scratch_shapes=[pltpu.VMEM((HEADS, LATENT, 128), bf16)],
        compiler_params=pltpu.CompilerParams(vmem_limit_bytes=VMEM_BYTES),
        cost_estimate=pl.CostEstimate(flops=9_000_000_000, bytes_accessed=4_200_000, transcendentals=8192),
        name="attention",
    )(
        pltpu.with_memory_space_constraint(q, pltpu.HBM),
        pltpu.with_memory_space_constraint(k, pltpu.HBM),
        lengths,
        up,
    )


def plan_kernel(routes_ref, score_ref, place_ref, weight_ref):
    routes, scores = routes_ref[...], score_ref[...]
    gates = 2.5 * scores / jnp.sum(scores, axis=0, keepdims=True)
    named = jnp.zeros((EXPERTS, ROWS), f32)
    gate = jnp.zeros((EXPERTS, ROWS), f32)
    for k in range(TOP):
        hit = iota((EXPERTS, ROWS), 0) == routes[k : k + 1, :]
        named += hit.astype(f32)
        gate += jnp.where(hit, gates[k : k + 1, :], 0.0)
    before = (iota((ROWS, ROWS), 0) < iota((ROWS, ROWS), 1)).astype(bf16)
    rank = mm(named.astype(bf16), before)

    spread = (iota((ROWS, 4 * ROWS), 1) % ROWS == iota((ROWS, 4 * ROWS), 0)).astype(bf16)
    expand = (iota((PIECES, EXPERTS), 0) // 8 == iota((PIECES, EXPERTS), 1)).astype(bf16)
    both = []
    for slot in range(2):
        here = jnp.where(rank == slot, named, 0.0).astype(bf16)
        both.append(mm(expand, mm(here, spread).astype(bf16)))
    n = iota((PIECES, 4 * ROWS), 0)
    place = jnp.where(n % 2 == 0, both[0], both[1])
    place_ref[...] = jnp.where(n % 8 // 2 == iota((PIECES, 4 * ROWS), 1) // ROWS, place, 0.0).astype(bf16)

    expand = (iota((EXPERTS, PIECES), 1) // 8 == iota((EXPERTS, PIECES), 0)).astype(bf16)
    n = iota((ROWS, PIECES), 1)
    high, low = [], []
    for slot in range(2):
        part = jnp.where(rank == slot, gate, 0.0).T
        top = part.astype(bf16)
        high.append(mm(top, expand))
        low.append(mm((part - top.astype(f32)).astype(bf16), expand))
    for i, parts in enumerate((high, low)):
        row = jnp.where(n % 2 == 0, parts[0], parts[1])
        for quarter in range(4):
            weight_ref[pl.ds((i * 4 + quarter) * ROWS, ROWS), :] = jnp.where(
                n % 8 // 2 == quarter, row, 0.0
            ).astype(bf16)


def plan(routes, scores):
    return pl.pallas_call(
        plan_kernel,
        out_shape=(
            jax.ShapeDtypeStruct((PIECES, 4 * ROWS), bf16),
            jax.ShapeDtypeStruct((8 * ROWS, PIECES), bf16),
        ),
        compiler_params=pltpu.CompilerParams(vmem_limit_bytes=VMEM_BYTES),
        cost_estimate=pl.CostEstimate(flops=60_000_000, bytes_accessed=500_000, transcendentals=0),
        name="plan",
    )(routes.T, scores.T)


def fetch_kernel(gain_ref, wi_ref, wo_ref, wi_out, wo_out, gain_out, sems):
    gain_out[...] = gain_ref[...]
    copies = []
    for source, target, pieces in ((wi_ref, wi_out, 8), (wo_ref, wo_out, 4)):
        depth = source.shape[0] // pieces
        for i in range(pieces):
            rows = pl.ds(i * depth, depth)
            copies.append(pltpu.make_async_copy(source.at[rows, :], target.at[rows, :], sems.at[len(copies)]))
    for copy in copies:
        copy.start()
    for copy in copies:
        copy.wait()


def fetch(gain, w_in, w_out):
    in_hbm = [pltpu.with_memory_space_constraint(w, pltpu.HBM) for w in (w_in, w_out)]
    return pl.pallas_call(
        fetch_kernel,
        in_specs=[pl.BlockSpec(memory_space=space) for space in (pltpu.VMEM, pltpu.HBM, pltpu.HBM)],
        out_specs=[pl.BlockSpec(memory_space=pltpu.VMEM)] * 3,
        out_shape=[
            pltpu.VMEM(w_in.shape, bf16),
            pltpu.VMEM(w_out.shape, bf16),
            jax.ShapeDtypeStruct((1, D), f32),
        ],
        scratch_shapes=[pltpu.SemaphoreType.DMA((12,))],
        compiler_params=pltpu.CompilerParams(vmem_limit_bytes=VMEM_BYTES),
        cost_estimate=pl.CostEstimate(flops=0, bytes_accessed=26_000_000, transcendentals=0),
        name="fetch",
    )(gain, *in_hbm)


def project_kernel(head_ref, other_ref, *refs):
    blocks, out_ref, (rows_ref, w_ref) = refs[:4], refs[6], refs[7:]
    for i in range(REQUESTS // ROWS):
        rows = slice(i * ROWS, (i + 1) * ROWS)
        rows_ref[2 * i * ROWS : (2 * i + 1) * ROWS, :] = head_ref[rows, :]
        rows_ref[(2 * i + 1) * ROWS : (2 * i + 2) * ROWS, :] = other_ref[rows, :]
    for i in range(4):
        w_ref[i * COLUMNS : (i + 1) * COLUMNS, :] = blocks[i][...]
    for i in range(2):
        columns = slice(i * 2 * COLUMNS, (i + 1) * 2 * COLUMNS)
        out_ref[:, columns] = lax.dot_general(
            rows_ref[...], w_ref[columns, :], (((1,), (1,)), ((), ())), preferred_element_type=f32
        ).astype(bf16)


def project(head_out, other_head, blocks, place, gain):
    return pl.pallas_call(
        project_kernel,
        in_specs=[pl.BlockSpec(memory_space=pltpu.VMEM)] * 8,
        out_specs=pl.BlockSpec(memory_space=pltpu.VMEM),
        out_shape=jax.ShapeDtypeStruct((2 * REQUESTS, 4 * COLUMNS), bf16),
        scratch_shapes=[
            pltpu.VMEM((2 * REQUESTS, HEADS * VALUE), bf16),
            pltpu.VMEM((4 * COLUMNS, HEADS * VALUE), bf16),
        ],
        compiler_params=pltpu.CompilerParams(vmem_limit_bytes=VMEM_BYTES),
        cost_estimate=pl.CostEstimate(flops=2 * REQUESTS * 512 * D, bytes_accessed=4_500_000, transcendentals=0),
        name="project",
    )(head_out, other_head, *blocks, place, gain)


def total_kernel(parts_ref, own_ref, other_ref):
    for out_ref, start in ((own_ref, 0), (other_ref, ROWS)):
        rows = slice(start, start + ROWS)
        total = parts_ref[0, rows, :].astype(f32)
        for i in range(1, parts_ref.shape[0]):
            total += parts_ref[i, rows, :].astype(f32)
        out_ref[...] = total.astype(bf16)


def total(parts):
    return pl.pallas_call(
        total_kernel,
        out_shape=[jax.ShapeDtypeStruct((ROWS, 4 * COLUMNS), bf16)] * 2,
        compiler_params=pltpu.CompilerParams(vmem_limit_bytes=VMEM_BYTES),
        cost_estimate=pl.CostEstimate(flops=1_000_000, bytes_accessed=2_000_000, transcendentals=0),
        name="total",
    )(parts)


def dispatch_kernel(own_ref, other_ref, res_ref, gain_ref, place_ref, hidden_ref, out_ref, norm_ref, sum_ref):
    z, core = lax.axis_index("z"), lax.axis_index("core")
    own, other = own_ref[...].astype(f32), other_ref[...].astype(f32)
    even = jnp.where(core == 0, own, other)
    odd = jnp.where(core == 0, other, own)
    for i, step in enumerate(CHIPS):
        columns = slice(i * COLUMNS, (i + 1) * COLUMNS)
        start = pl.multiple_of(lax.rem(z + step, 4) * QUARTER, 128)
        sum_ref[:, pl.ds(start, QUARTER)] = jnp.concatenate([even[:, columns], odd[:, columns]], axis=1)
    hidden = (res_ref[...].astype(f32) + sum_ref[...]).astype(bf16)
    hidden_ref[...] = hidden
    hidden = hidden.astype(f32)
    inverse = lax.rsqrt(jnp.mean(hidden * hidden, axis=1, keepdims=True) + 1e-6)
    normed = (hidden * inverse * gain_ref[...]).astype(bf16)
    for quarter in range(4):
        norm_ref[pl.ds(quarter * ROWS, ROWS), :] = normed[:, quarter * QUARTER : (quarter + 1) * QUARTER]

    for start in range(0, PIECES, PIECES // 4):
        rows = slice(start, start + PIECES // 4)
        out_ref[rows, :] = mm(place_ref[rows, :], norm_ref[...]).astype(bf16)


def dispatch(own, other, residual, gain, place):
    return pl.pallas_call(
        dispatch_kernel,
        out_shape=(
            jax.ShapeDtypeStruct((ROWS, D), bf16),
            jax.ShapeDtypeStruct((PIECES, QUARTER), bf16),
        ),
        scratch_shapes=[pltpu.VMEM((4 * ROWS, QUARTER), bf16), pltpu.VMEM((ROWS, D), f32)],
        compiler_params=pltpu.CompilerParams(vmem_limit_bytes=VMEM_BYTES),
        cost_estimate=pl.CostEstimate(flops=120_000_000, bytes_accessed=4_000_000, transcendentals=16),
        name="dispatch",
    )(own, other, residual, gain, place)


def expert_kernel(x_ref, wi_ref, wo_ref, out_ref, rows_ref, act_ref, back_ref):
    half = FF // 2

    def matches(to, frm):
        same_quarter = to // 64 == frm % 8 // 2
        return (same_quarter & (to % 64 // 2 == frm // 8) & (to % 2 == frm % 2)).astype(bf16)

    sort = matches(iota((256, 256), 0), iota((256, 256), 1))
    unsort = matches(iota((256, 256), 1), iota((256, 256), 0))
    for pair in range(2):
        blocks = [x_ref[b * 256 : (b + 1) * 256, :] for b in (2 * pair, 2 * pair + 1)]
        sorted_rows = mm(sort, jnp.concatenate(blocks, axis=1)).astype(bf16)
        for i in range(2):
            start = (2 * pair + i) * 64
            for quarter in range(4):
                rows_ref[start : start + 64, quarter * QUARTER : (quarter + 1) * QUARTER] = sorted_rows[
                    quarter * 64 : (quarter + 1) * 64, i * QUARTER : (i + 1) * QUARTER
                ]

    for i in range(2):
        gate = mm(rows_ref[...], wi_ref[:, i * half : (i + 1) * half])
        up = mm(rows_ref[...], wi_ref[:, FF + i * half : FF + (i + 1) * half])
        act_ref[:, i * half : (i + 1) * half] = (jax.nn.silu(gate) * up).astype(bf16)

    for pair in range(2):
        result = mm(act_ref[...], wo_ref[:, pair * 2 * QUARTER : (pair + 1) * 2 * QUARTER]).astype(bf16)
        for i in range(2):
            rows = slice((2 * pair + i) * 64, (2 * pair + i + 1) * 64)
            for b in range(4):
                columns = slice(b % 2 * QUARTER, (b % 2 + 1) * QUARTER)
                back_ref[b // 2, rows, columns] = result[
                    b * 64 : (b + 1) * 64, i * QUARTER : (i + 1) * QUARTER
                ]
    for pair in range(2):
        result = mm(unsort, back_ref[pair]).astype(bf16)
        for i in range(2):
            start = (2 * pair + i) * 256
            out_ref[start : start + 256, :] = result[:, i * QUARTER : (i + 1) * QUARTER]


def expert(pieces, w_in, w_out):
    rows = 2 * EXPERTS
    return pl.pallas_call(
        expert_kernel,
        in_specs=[pl.BlockSpec(memory_space=pltpu.VMEM)] * 3,
        out_specs=pl.BlockSpec(memory_space=pltpu.VMEM),
        out_shape=jax.ShapeDtypeStruct((PIECES, QUARTER), bf16),
        scratch_shapes=[
            pltpu.VMEM((rows, D), bf16),
            pltpu.VMEM((rows, FF), bf16),
            pltpu.VMEM((2, 256, 2 * QUARTER), bf16),
        ],
        compiler_params=pltpu.CompilerParams(vmem_limit_bytes=VMEM_BYTES),
        cost_estimate=pl.CostEstimate(
            flops=2 * rows * 3 * D * FF, bytes_accessed=26_000_000, transcendentals=rows * FF
        ),
        name="expert",
    )(
        pieces,
        w_in,
        w_out,
    )


def combine_kernel(back_ref, weight_ref, hidden_ref, out_ref):
    both = mm(weight_ref[...], back_ref[...])
    for quarter in range(4):
        columns = slice(quarter * QUARTER, (quarter + 1) * QUARTER)
        rows = slice(quarter * ROWS, (quarter + 1) * ROWS)
        low_rows = slice((4 + quarter) * ROWS, (5 + quarter) * ROWS)
        out_ref[:, columns] = (hidden_ref[:, columns].astype(f32) + (both[rows] + both[low_rows])).astype(bf16)


def combine(back, weight, hidden):
    return pl.pallas_call(
        combine_kernel,
        out_shape=jax.ShapeDtypeStruct((ROWS, D), bf16),
        compiler_params=pltpu.CompilerParams(vmem_limit_bytes=VMEM_BYTES),
        cost_estimate=pl.CostEstimate(flops=240_000_000, bytes_accessed=2_400_000, transcendentals=0),
        name="combine",
    )(back, weight, hidden)


def local(
    queries,
    cached_latent_rows,
    lengths,
    value_up_weight,
    out_proj,
    residual_in,
    norm_gain,
    routes,
    route_scores,
    w_gate_up,
    w_down,
):
    own = out_proj.T
    others = [lax.ppermute(own, "z", [(i, (i - step) % 4) for i in range(4)]) for step in CHIPS[1:]]
    def other_core(block):
        return lax.ppermute(block, "core", [(0, 1), (1, 0)])

    head_out = attention(
        queries.transpose(1, 2, 0),
        cached_latent_rows.transpose(1, 2, 0),
        lengths.reshape(1, REQUESTS),
        value_up_weight,
    )
    place, weight = plan(routes, route_scores)
    w_in, w_out, gain = fetch(norm_gain.reshape(1, D), w_gate_up[0], w_down[0])
    shares = project(head_out, other_core(head_out), (own, *others), place, gain)
    parts = lax.all_to_all(
        shares.reshape(16, 2 * ROWS, 4 * COLUMNS), ("y", "x"), split_axis=0, concat_axis=0, tiled=True
    )
    own_total, other_total = total(parts)
    hidden, outgoing = dispatch(own_total, other_core(other_total), residual_in, gain, place)
    everyone = ("z", "core", "y", "x")
    arrived = lax.all_to_all(
        outgoing.reshape(EXPERTS, 8, QUARTER), everyone, split_axis=0, concat_axis=0, tiled=True
    )
    produced = expert(arrived.reshape(PIECES, QUARTER), w_in, w_out)
    returned = lax.all_to_all(
        produced.reshape(EXPERTS, 8, QUARTER), everyone, split_axis=0, concat_axis=0, tiled=True
    )
    return combine(returned.reshape(PIECES, QUARTER), weight, hidden)


def solution(mesh):
    fine = Mesh(mesh.devices.reshape(4, 2, 4, 4), ("z", "core", "y", "x"))
    dp, ex, both = ("z", "core"), ("y", "x"), ("z", "core", "y", "x")
    in_specs = (
        P(dp, ex, None),
        P(dp, None, None),
        P(dp),
        P(ex, None, None),
        P(ex, dp),
        P(both, None),
        P(),
        P(both, None),
        P(both, None),
        P(both, None, None),
        P(both, None, None),
    )
    return jax.shard_map(local, mesh=fine, in_specs=in_specs, out_specs=P(both, None), check_vma=False)
```

```python
import jax
import jax.numpy as jnp
from jax import lax
from jax.experimental import pallas as pl
from jax.experimental.pallas import tpu as pltpu
from jax.sharding import Mesh, PartitionSpec as P

D = 3584
FF = 1024
HEADS = 4
LATENT = 512
WIDTH = 576
VALUE = 128
SLOTS = 8
TOP = 8
EXPERTS = 128
ROWS = 16
REQUESTS = 256
QUARTER = D // 4
PIECES = EXPERTS * 8
COLUMNS = 448
CHIPS = (0, 2, 1, 3)

score_scale = 0.07216878364870323

f32, bf16 = jnp.float32, jnp.bfloat16
VMEM_BYTES = 16 * 1024 * 1024


def iota(shape, dim):
    return lax.broadcasted_iota(jnp.int32, shape, dim)


def mm(a, b):
    return jnp.dot(a, b, preferred_element_type=f32)


def attention_kernel(q_ref, k_ref, len_ref, up_ref, out_ref, lat_ref):
    def score_step(i, sums):
        rows = pl.ds(i * 16, 16)
        q = [q_ref[h, rows, :].astype(f32) for h in range(HEADS)]
        k = [k_ref[s, rows, :].astype(f32) for s in range(SLOTS)]
        new = []
        for h in range(HEADS):
            for s in range(SLOTS):
                prod = q[h] * k[s]
                new.append(sums[h * SLOTS + s] + (prod[:8] + prod[8:]))
        return tuple(new)

    sums = lax.fori_loop(
        0, WIDTH // 16, score_step, tuple(jnp.zeros((8, 128), f32) for _ in range(HEADS * SLOTS))
    )
    live = iota((SLOTS, 128), 0) < len_ref[...]
    probs = []
    for h in range(HEADS):
        scores = jnp.concatenate(
            [jnp.sum(sums[h * SLOTS + s], axis=0, keepdims=True) for s in range(SLOTS)], axis=0
        )
        scores = jnp.where(live, scores * score_scale, -1e30)
        expo = jnp.exp(scores - jnp.max(scores, axis=0, keepdims=True))
        prob = (expo / jnp.sum(expo, axis=0, keepdims=True)).astype(bf16).astype(f32)
        probs.append([jnp.broadcast_to(prob[s : s + 1], (8, 128)) for s in range(SLOTS)])

    @pl.loop(0, LATENT // 16)
    def _(i):
        rows = pl.ds(i * 16, 16)
        k = [k_ref[s, rows, :].astype(f32) for s in range(SLOTS)]
        for h in range(HEADS):
            low = sum(probs[h][s] * k[s][:8] for s in range(SLOTS))
            high = sum(probs[h][s] * k[s][8:] for s in range(SLOTS))
            lat_ref[h, rows, :] = jnp.concatenate([low, high], axis=0).astype(bf16)

    for h in range(HEADS):
        out_ref[:, h * VALUE : (h + 1) * VALUE] = lax.dot_general(
            lat_ref[h], up_ref[h], (((0,), (0,)), ((), ())), preferred_element_type=f32
        ).astype(bf16)


def attention(q, k, lengths, up):
    return pl.pallas_call(
        attention_kernel,
        grid=(REQUESTS // 128,),
        in_specs=[
            pl.BlockSpec((HEADS, WIDTH, 128), lambda j: (0, 0, j)),
            pl.BlockSpec((SLOTS, WIDTH, 128), lambda j: (0, 0, j)),
            pl.BlockSpec((1, 128), lambda j: (0, j)),
            pl.BlockSpec((HEADS, LATENT, VALUE), lambda j: (0, 0, 0)),
        ],
        out_specs=pl.BlockSpec((128, HEADS * VALUE), lambda j: (j, 0)),
        out_shape=jax.ShapeDtypeStruct((REQUESTS, HEADS * VALUE), bf16),
        scratch_shapes=[pltpu.VMEM((HEADS, LATENT, 128), bf16)],
        compiler_params=pltpu.CompilerParams(vmem_limit_bytes=VMEM_BYTES),
        cost_estimate=pl.CostEstimate(flops=9_000_000_000, bytes_accessed=4_200_000, transcendentals=8192),
        name="attention",
    )(
        pltpu.with_memory_space_constraint(q, pltpu.HBM),
        pltpu.with_memory_space_constraint(k, pltpu.HBM),
        lengths,
        up,
    )


def plan_kernel(routes_ref, score_ref, place_ref, weight_ref, sort_ref, unsort_ref):
    def matches(to, frm):
        same_quarter = to // 64 == frm % 8 // 2
        return (same_quarter & (to % 64 // 2 == frm // 8) & (to % 2 == frm % 2)).astype(bf16)

    sort_ref[...] = matches(iota((256, 256), 0), iota((256, 256), 1))
    unsort_ref[...] = matches(iota((256, 256), 1), iota((256, 256), 0))

    routes, scores = routes_ref[...], score_ref[...]
    gates = 2.5 * scores / jnp.sum(scores, axis=0, keepdims=True)
    named = jnp.zeros((EXPERTS, ROWS), f32)
    gate = jnp.zeros((EXPERTS, ROWS), f32)
    for k in range(TOP):
        hit = iota((EXPERTS, ROWS), 0) == routes[k : k + 1, :]
        named += hit.astype(f32)
        gate += jnp.where(hit, gates[k : k + 1, :], 0.0)
    before = (iota((ROWS, ROWS), 0) < iota((ROWS, ROWS), 1)).astype(bf16)
    rank = mm(named.astype(bf16), before)

    spread = (iota((ROWS, 4 * ROWS), 1) % ROWS == iota((ROWS, 4 * ROWS), 0)).astype(bf16)
    expand = (iota((PIECES, EXPERTS), 0) // 8 == iota((PIECES, EXPERTS), 1)).astype(bf16)
    both = []
    for slot in range(2):
        here = jnp.where(rank == slot, named, 0.0).astype(bf16)
        both.append(mm(expand, mm(here, spread).astype(bf16)))
    n = iota((PIECES, 4 * ROWS), 0)
    place = jnp.where(n % 2 == 0, both[0], both[1])
    place_ref[...] = jnp.where(n % 8 // 2 == iota((PIECES, 4 * ROWS), 1) // ROWS, place, 0.0).astype(bf16)

    expand = (iota((EXPERTS, PIECES), 1) // 8 == iota((EXPERTS, PIECES), 0)).astype(bf16)
    n = iota((ROWS, PIECES), 1)
    high, low = [], []
    for slot in range(2):
        part = jnp.where(rank == slot, gate, 0.0).T
        top = part.astype(bf16)
        high.append(mm(top, expand))
        low.append(mm((part - top.astype(f32)).astype(bf16), expand))
    for i, parts in enumerate((high, low)):
        row = jnp.where(n % 2 == 0, parts[0], parts[1])
        for quarter in range(4):
            weight_ref[pl.ds((i * 4 + quarter) * ROWS, ROWS), :] = jnp.where(
                n % 8 // 2 == quarter, row, 0.0
            ).astype(bf16)


def plan(routes, scores):
    return pl.pallas_call(
        plan_kernel,
        out_shape=(
            jax.ShapeDtypeStruct((PIECES, 4 * ROWS), bf16),
            jax.ShapeDtypeStruct((8 * ROWS, PIECES), bf16),
            jax.ShapeDtypeStruct((256, 256), bf16),
            jax.ShapeDtypeStruct((256, 256), bf16),
        ),
        compiler_params=pltpu.CompilerParams(vmem_limit_bytes=VMEM_BYTES),
        cost_estimate=pl.CostEstimate(flops=60_000_000, bytes_accessed=500_000, transcendentals=0),
        name="plan",
    )(routes.T, scores.T)


def fetch_kernel(gain_ref, wi_ref, wo_ref, wi_out, wo_out, gain_out, sems):
    gain_out[...] = gain_ref[...]
    copies = []
    for source, target, pieces in ((wi_ref, wi_out, 8), (wo_ref, wo_out, 4)):
        depth = source.shape[0] // pieces
        for i in range(pieces):
            rows = pl.ds(i * depth, depth)
            copies.append(pltpu.make_async_copy(source.at[rows, :], target.at[rows, :], sems.at[len(copies)]))
    for copy in copies:
        copy.start()
    for copy in copies:
        copy.wait()


def fetch(gain, w_in, w_out):
    in_hbm = [pltpu.with_memory_space_constraint(w, pltpu.HBM) for w in (w_in, w_out)]
    return pl.pallas_call(
        fetch_kernel,
        in_specs=[pl.BlockSpec(memory_space=space) for space in (pltpu.VMEM, pltpu.HBM, pltpu.HBM)],
        out_specs=[pl.BlockSpec(memory_space=pltpu.VMEM)] * 3,
        out_shape=[
            pltpu.VMEM(w_in.shape, bf16),
            pltpu.VMEM(w_out.shape, bf16),
            jax.ShapeDtypeStruct((1, D), f32),
        ],
        scratch_shapes=[pltpu.SemaphoreType.DMA((12,))],
        compiler_params=pltpu.CompilerParams(vmem_limit_bytes=VMEM_BYTES),
        cost_estimate=pl.CostEstimate(flops=0, bytes_accessed=26_000_000, transcendentals=0),
        name="fetch",
    )(gain, *in_hbm)


def project_kernel(head_ref, other_ref, *refs):
    blocks, out_ref, (rows_ref, w_ref) = refs[:4], refs[6], refs[7:]
    for i in range(REQUESTS // ROWS):
        rows = slice(i * ROWS, (i + 1) * ROWS)
        rows_ref[2 * i * ROWS : (2 * i + 1) * ROWS, :] = head_ref[rows, :]
        rows_ref[(2 * i + 1) * ROWS : (2 * i + 2) * ROWS, :] = other_ref[rows, :]
    for i in range(4):
        w_ref[i * COLUMNS : (i + 1) * COLUMNS, :] = blocks[i][...]
    for i in range(2):
        columns = slice(i * 2 * COLUMNS, (i + 1) * 2 * COLUMNS)
        out_ref[:, columns] = lax.dot_general(
            rows_ref[...], w_ref[columns, :], (((1,), (1,)), ((), ())), preferred_element_type=f32
        ).astype(bf16)


def project(head_out, other_head, blocks, place, gain):
    return pl.pallas_call(
        project_kernel,
        in_specs=[pl.BlockSpec(memory_space=pltpu.VMEM)] * 8,
        out_specs=pl.BlockSpec(memory_space=pltpu.VMEM),
        out_shape=jax.ShapeDtypeStruct((2 * REQUESTS, 4 * COLUMNS), bf16),
        scratch_shapes=[
            pltpu.VMEM((2 * REQUESTS, HEADS * VALUE), bf16),
            pltpu.VMEM((4 * COLUMNS, HEADS * VALUE), bf16),
        ],
        compiler_params=pltpu.CompilerParams(vmem_limit_bytes=VMEM_BYTES),
        cost_estimate=pl.CostEstimate(flops=2 * REQUESTS * 512 * D, bytes_accessed=4_500_000, transcendentals=0),
        name="project",
    )(head_out, other_head, *blocks, place, gain)


def total_kernel(parts_ref, own_ref, other_ref):
    for out_ref, start in ((own_ref, 0), (other_ref, ROWS)):
        rows = slice(start, start + ROWS)
        total = parts_ref[0, rows, :].astype(f32)
        for i in range(1, parts_ref.shape[0]):
            total += parts_ref[i, rows, :].astype(f32)
        out_ref[...] = total.astype(bf16)


def total(parts):
    return pl.pallas_call(
        total_kernel,
        out_shape=[jax.ShapeDtypeStruct((ROWS, 4 * COLUMNS), bf16)] * 2,
        compiler_params=pltpu.CompilerParams(vmem_limit_bytes=VMEM_BYTES),
        cost_estimate=pl.CostEstimate(flops=1_000_000, bytes_accessed=2_000_000, transcendentals=0),
        name="total",
    )(parts)


def dispatch_kernel(own_ref, other_ref, res_ref, gain_ref, place_ref, hidden_ref, out_ref, norm_ref, sum_ref):
    z, core = lax.axis_index("z"), lax.axis_index("core")
    own, other = own_ref[...].astype(f32), other_ref[...].astype(f32)
    even = jnp.where(core == 0, own, other)
    odd = jnp.where(core == 0, other, own)
    for i, step in enumerate(CHIPS):
        columns = slice(i * COLUMNS, (i + 1) * COLUMNS)
        start = pl.multiple_of(lax.rem(z + step, 4) * QUARTER, 128)
        sum_ref[:, pl.ds(start, QUARTER)] = jnp.concatenate([even[:, columns], odd[:, columns]], axis=1)
    hidden = (res_ref[...].astype(f32) + sum_ref[...]).astype(bf16)
    hidden_ref[...] = hidden
    hidden = hidden.astype(f32)
    inverse = lax.rsqrt(jnp.mean(hidden * hidden, axis=1, keepdims=True) + 1e-6)
    normed = (hidden * inverse * gain_ref[...]).astype(bf16)
    for quarter in range(4):
        norm_ref[pl.ds(quarter * ROWS, ROWS), :] = normed[:, quarter * QUARTER : (quarter + 1) * QUARTER]

    for start in range(0, PIECES, PIECES // 4):
        rows = slice(start, start + PIECES // 4)
        out_ref[rows, :] = mm(place_ref[rows, :], norm_ref[...]).astype(bf16)


def dispatch(own, other, residual, gain, place):
    return pl.pallas_call(
        dispatch_kernel,
        out_shape=(
            jax.ShapeDtypeStruct((ROWS, D), bf16),
            jax.ShapeDtypeStruct((PIECES, QUARTER), bf16),
        ),
        scratch_shapes=[pltpu.VMEM((4 * ROWS, QUARTER), bf16), pltpu.VMEM((ROWS, D), f32)],
        compiler_params=pltpu.CompilerParams(vmem_limit_bytes=VMEM_BYTES),
        cost_estimate=pl.CostEstimate(flops=120_000_000, bytes_accessed=4_000_000, transcendentals=16),
        name="dispatch",
    )(own, other, residual, gain, place)


def expert_kernel(x_ref, wi_ref, wo_ref, sort_ref, unsort_ref, out_ref, rows_ref, act_ref, back_ref):
    half = FF // 2

    for pair in range(2):
        blocks = [x_ref[b * 256 : (b + 1) * 256, :] for b in (2 * pair, 2 * pair + 1)]
        sorted_rows = mm(sort_ref[...], jnp.concatenate(blocks, axis=1)).astype(bf16)
        for i in range(2):
            start = (2 * pair + i) * 64
            for quarter in range(4):
                rows_ref[start : start + 64, quarter * QUARTER : (quarter + 1) * QUARTER] = sorted_rows[
                    quarter * 64 : (quarter + 1) * 64, i * QUARTER : (i + 1) * QUARTER
                ]

    for i in range(2):
        gate = mm(rows_ref[...], wi_ref[:, i * half : (i + 1) * half])
        up = mm(rows_ref[...], wi_ref[:, FF + i * half : FF + (i + 1) * half])
        act_ref[:, i * half : (i + 1) * half] = (jax.nn.silu(gate) * up).astype(bf16)

    for pair in range(2):
        result = mm(act_ref[...], wo_ref[:, pair * 2 * QUARTER : (pair + 1) * 2 * QUARTER]).astype(bf16)
        for i in range(2):
            rows = slice((2 * pair + i) * 64, (2 * pair + i + 1) * 64)
            for b in range(4):
                columns = slice(b % 2 * QUARTER, (b % 2 + 1) * QUARTER)
                back_ref[b // 2, rows, columns] = result[
                    b * 64 : (b + 1) * 64, i * QUARTER : (i + 1) * QUARTER
                ]
    for pair in range(2):
        result = mm(unsort_ref[...], back_ref[pair]).astype(bf16)
        for i in range(2):
            start = (2 * pair + i) * 256
            out_ref[start : start + 256, :] = result[:, i * QUARTER : (i + 1) * QUARTER]


def expert(pieces, w_in, w_out, sort, unsort):
    rows = 2 * EXPERTS
    return pl.pallas_call(
        expert_kernel,
        in_specs=[pl.BlockSpec(memory_space=pltpu.VMEM)] * 5,
        out_specs=pl.BlockSpec(memory_space=pltpu.VMEM),
        out_shape=jax.ShapeDtypeStruct((PIECES, QUARTER), bf16),
        scratch_shapes=[
            pltpu.VMEM((rows, D), bf16),
            pltpu.VMEM((rows, FF), bf16),
            pltpu.VMEM((2, 256, 2 * QUARTER), bf16),
        ],
        compiler_params=pltpu.CompilerParams(vmem_limit_bytes=VMEM_BYTES),
        cost_estimate=pl.CostEstimate(
            flops=2 * rows * 3 * D * FF, bytes_accessed=26_000_000, transcendentals=rows * FF
        ),
        name="expert",
    )(
        pieces,
        w_in,
        w_out,
        sort,
        unsort,
    )


def combine_kernel(back_ref, weight_ref, hidden_ref, out_ref):
    both = mm(weight_ref[...], back_ref[...])
    for quarter in range(4):
        columns = slice(quarter * QUARTER, (quarter + 1) * QUARTER)
        rows = slice(quarter * ROWS, (quarter + 1) * ROWS)
        low_rows = slice((4 + quarter) * ROWS, (5 + quarter) * ROWS)
        out_ref[:, columns] = (hidden_ref[:, columns].astype(f32) + (both[rows] + both[low_rows])).astype(bf16)


def combine(back, weight, hidden):
    return pl.pallas_call(
        combine_kernel,
        out_shape=jax.ShapeDtypeStruct((ROWS, D), bf16),
        compiler_params=pltpu.CompilerParams(vmem_limit_bytes=VMEM_BYTES),
        cost_estimate=pl.CostEstimate(flops=240_000_000, bytes_accessed=2_400_000, transcendentals=0),
        name="combine",
    )(back, weight, hidden)


def local(
    queries,
    cached_latent_rows,
    lengths,
    value_up_weight,
    out_proj,
    residual_in,
    norm_gain,
    routes,
    route_scores,
    w_gate_up,
    w_down,
):
    own = out_proj.T
    others = [lax.ppermute(own, "z", [(i, (i - step) % 4) for i in range(4)]) for step in CHIPS[1:]]
    def other_core(block):
        return lax.ppermute(block, "core", [(0, 1), (1, 0)])

    head_out = attention(
        queries.transpose(1, 2, 0),
        cached_latent_rows.transpose(1, 2, 0),
        lengths.reshape(1, REQUESTS),
        value_up_weight,
    )
    place, weight, sort, unsort = plan(routes, route_scores)
    w_in, w_out, gain = fetch(norm_gain.reshape(1, D), w_gate_up[0], w_down[0])
    shares = project(head_out, other_core(head_out), (own, *others), place, gain)
    parts = lax.all_to_all(
        shares.reshape(16, 2 * ROWS, 4 * COLUMNS), ("y", "x"), split_axis=0, concat_axis=0, tiled=True
    )
    own_total, other_total = total(parts)
    hidden, outgoing = dispatch(own_total, other_core(other_total), residual_in, gain, place)
    everyone = ("z", "core", "y", "x")
    arrived = lax.all_to_all(
        outgoing.reshape(EXPERTS, 8, QUARTER), everyone, split_axis=0, concat_axis=0, tiled=True
    )
    produced = expert(arrived.reshape(PIECES, QUARTER), w_in, w_out, sort, unsort)
    returned = lax.all_to_all(
        produced.reshape(EXPERTS, 8, QUARTER), everyone, split_axis=0, concat_axis=0, tiled=True
    )
    return combine(returned.reshape(PIECES, QUARTER), weight, hidden)


def solution(mesh):
    fine = Mesh(mesh.devices.reshape(4, 2, 4, 4), ("z", "core", "y", "x"))
    dp, ex, both = ("z", "core"), ("y", "x"), ("z", "core", "y", "x")
    in_specs = (
        P(dp, ex, None),
        P(dp, None, None),
        P(dp),
        P(ex, None, None),
        P(ex, dp),
        P(both, None),
        P(),
        P(both, None),
        P(both, None),
        P(both, None, None),
        P(both, None, None),
    )
    return jax.shard_map(local, mesh=fine, in_specs=in_specs, out_specs=P(both, None), check_vma=False)
```
